256 devices in a mesh: prefix: 32 (over z, y), samples: 8 (over x, core).
Axes of the slice: x: 4, y: 4, z: 8, core: 2. Of those that a mesh axis runs over, the one named last changes fastest.
Arguments:
- query: bfloat16 [256, 8192], P(('samples', 'prefix')), may hold values from -192 to 192
- prompt_code_cache: bfloat16 [2, 65536, 8, 128], P(None, 'prefix'), may hold values from -127 to 127
- prompt_scale_cache: bfloat16 [2, 1024, 8], P(None, 'prefix'), may hold values from 0.00390625 to 0.015625, as said below
- prefix_len: int32 [1], replicated, may hold values from 32768 to 65536
- sample_key_value_cache: bfloat16 [256, 2, 512, 1024], P(('samples', 'prefix')), may hold values from -9 to 9
- suffix_len: int32 [256], P(('samples', 'prefix')), may hold values from 1 to 512, 65536 in all
- w_out: bfloat16 [8192, 8192], P('prefix', 'samples'), may hold values from -0.0625 to 0.0625
Outputs:
- mixed: bfloat16 [256, 8192], P('prefix', 'samples')
The draws below stay inside these ranges and needn't reach their ends.
Inputs may be any that keep to these rules, and one draw needn't show every extreme that they name: `prompt_scale_cache`: each scale is 2 ** -8, 2 ** -7 or 2 ** -6. `suffix_len`: some sample uses all 512 positions.
All inputs are finite; a program needn't handle non-finite values. No bound on the sum of `suffix_len` on one device may be relied on, other than what follows from the above.
Results may differ from the reference program's by a relative error of at most 0.0075.
Values may be sent and summed in bfloat16 or wider, within the bound.
No kernel may reach another device: no remote copies, remote signals or barrier semaphores. Data moves between devices by JAX's collectives and lax.ppermute only.
A program may use at most 192 MiB of HBM per device.

```python
import math
import jax
import jax.numpy as jnp
import numpy as np
from jax import lax

QUERY_HEADS = 64
KEY_VALUE_HEADS = 8
HEAD_SIZE = 128
D = 8192
PROMPT_PER_INDEX = 2048
CONTINUE_MAX = 512
SCALE_BLOCK = 64
PROMPT_TOTAL = 65536
SAMPLE_COUNT = 256
N_PREFIX = 32


def draw_query(key, part):
    key = jax.random.fold_in(key, 11)
    noise_random_key = jax.random.fold_in(key, 0)
    random_noise = jax.random.normal(noise_random_key, (SAMPLE_COUNT, KEY_VALUE_HEADS, QUERY_HEADS // KEY_VALUE_HEADS, HEAD_SIZE), jnp.float32)
    value_rows = jnp.clip(2.0 * random_noise, -12.0, 12.0)
    return value_rows.reshape(SAMPLE_COUNT, QUERY_HEADS * HEAD_SIZE).astype(jnp.bfloat16)


def draw_prompt_code_cache(key, part):
    key = jax.random.fold_in(key, 23)
    random_key_third = jax.random.fold_in(key, 2)
    value_rows = jax.random.randint(random_key_third, (2, PROMPT_TOTAL, KEY_VALUE_HEADS, HEAD_SIZE), -127, 128)
    return value_rows.astype(jnp.float32).astype(jnp.bfloat16)


def draw_prompt_scale_cache(key, part):
    key = jax.random.fold_in(key, 37)
    choices_table = jnp.array([0.00390625, 0.0078125, 0.015625], jnp.float32)
    picked = jax.random.randint(key, (2, PROMPT_TOTAL // SCALE_BLOCK, KEY_VALUE_HEADS), 0, 3)
    return choices_table[picked].astype(jnp.bfloat16)


def level_of(own_key, shape, pieces, least, largest):
    def one(dim, parts):
        steps = jax.random.uniform(jax.random.fold_in(jax.random.fold_in(own_key, 6), dim), (parts,), jnp.float32, least / len(pieces), largest / len(pieces))
        return jnp.repeat(jnp.exp(steps), shape[dim] // parts).reshape((-1,) + (1,) * (len(shape) - dim - 1))

    factor_of = one(*pieces[0])
    for cut in pieces[1:]:
        factor_of = factor_of * one(*cut)
    return factor_of


def length_profile(number_of, total, bound, lean):
    weights = [(1 << 20) // math.isqrt(rank ** lean) + 1 for rank in range(2, number_of + 1)]
    spare, given = total - bound - (number_of - 1), [1] * (number_of - 1)
    while spare > 0:
        movable = [i for i in range(number_of - 1) if given[i] < bound]
        whole, budget = sum([weights[i] for i in movable]), spare
        for i in movable:
            extra = min(bound - given[i], max(1, budget * weights[i] // whole), spare)
            given[i] = given[i] + extra
            spare = spare - extra
    return np.array([bound] + given)


def ragged(stream_key, amount, total, reach, lean):
    if amount == 2:
        one = jax.random.randint(stream_key, (), max(1, total - reach), min(reach, total - 1) + 1)
        return jnp.stack([one, total - one])
    lengths = jnp.asarray(length_profile(amount, total, reach, lean), jnp.int32)
    couples = (amount - 1) // 2
    giver, sink = lengths[1:1 + 2 * couples:2], lengths[2:2 + 2 * couples:2]
    margin = jnp.minimum(giver - 1, reach - sink)
    passed = jax.random.randint(jax.random.fold_in(stream_key, 1), (couples,), 0, 1 << 20) % (margin + 1)
    lengths = lengths.at[1:1 + 2 * couples:2].set(giver - passed).at[2:2 + 2 * couples:2].set(sink + passed)
    return lengths[jax.random.permutation(jax.random.fold_in(stream_key, 2), amount)]


def noise(rng, extent, deviation, bound, shards=(), held_as=jnp.bfloat16):
    loudness = level_of(rng, extent, shards, -0.22, 0.18) if shards else 1.0
    values = jax.random.normal(rng, extent, jnp.float32) * deviation * loudness
    return jnp.minimum(jnp.maximum(values, -bound), bound).astype(held_as)


def setup_inputs(seed: int = 0) -> dict:
    streams_of = jax.random.split(jax.random.key(seed), 8)
    return {
        "query": draw_query(jax.random.fold_in(streams_of[7], 71), 0),
        "prompt_code_cache": draw_prompt_code_cache(jax.random.fold_in(streams_of[7], 71), 0),
        "prompt_scale_cache": draw_prompt_scale_cache(jax.random.fold_in(streams_of[7], 71), 0),
        "prefix_len": jax.random.randint(streams_of[3], (1,), PROMPT_TOTAL // 2, PROMPT_TOTAL + 1).astype(jnp.int32),
        "sample_key_value_cache": noise(streams_of[4], (SAMPLE_COUNT, 2, CONTINUE_MAX, KEY_VALUE_HEADS * HEAD_SIZE), 1.5, 9.0, ((0, 256),)),
        "suffix_len": ragged(streams_of[5], SAMPLE_COUNT, SAMPLE_COUNT * CONTINUE_MAX // 2, CONTINUE_MAX, 2).astype(jnp.int32),
        "w_out": noise(streams_of[6], (QUERY_HEADS * HEAD_SIZE, D), (QUERY_HEADS * HEAD_SIZE) ** -0.5, 0.0625, ((0, 32), (1, 8))),
    }


def attend_block(query_rows, key_rows, value_rows, valid, scale):
    scores = jnp.einsum('sjgd,tjd->sjgt', query_rows.astype(jnp.float32), key_rows.astype(jnp.float32)) * scale
    scores = jnp.where(valid, scores, -jnp.inf)
    top = lax.optimization_barrier(jnp.max(scores, axis=-1))
    safe = jnp.where(top == -jnp.inf, 0.0, top)
    weights = jnp.exp(scores - safe[..., None]).astype(jnp.bfloat16)
    total = lax.optimization_barrier(jnp.sum(weights.astype(jnp.float32), axis=-1))
    out = jnp.einsum('sjgt,tjd->sjgd', weights.astype(jnp.float32), value_rows.astype(jnp.float32))
    return (out, top, total)

def reference(query, prompt_code_cache, prompt_scale_cache, prefix_len, sample_key_value_cache, suffix_len, w_out):
    query_group = QUERY_HEADS // KEY_VALUE_HEADS
    scale = 1.0 / math.sqrt(HEAD_SIZE)
    query_rows = query.reshape(SAMPLE_COUNT, KEY_VALUE_HEADS, query_group, HEAD_SIZE)
    block_count = PROMPT_PER_INDEX // SCALE_BLOCK

    def one_block(index):
        start = (index * PROMPT_PER_INDEX).astype(jnp.int32)
        code_values = lax.dynamic_slice_in_dim(prompt_code_cache, start, PROMPT_PER_INDEX, 1)
        scale_values = lax.dynamic_slice_in_dim(prompt_scale_cache, (index * block_count).astype(jnp.int32), block_count, 1)
        matrix_product = code_values.astype(jnp.float32).reshape(2, block_count, SCALE_BLOCK, KEY_VALUE_HEADS, HEAD_SIZE) * scale_values.astype(jnp.float32)[:, :, None, :, None]
        restored_cache = matrix_product.astype(jnp.bfloat16).reshape(2, PROMPT_PER_INDEX, KEY_VALUE_HEADS, HEAD_SIZE)
        positions = start + jnp.arange(PROMPT_PER_INDEX, dtype=jnp.int32)
        valid = (positions < prefix_len[0])[None, None, None, :]
        return attend_block(query_rows, restored_cache[0], restored_cache[1], valid, scale)
    block_out, block_top, block_total = lax.map(one_block, jnp.arange(N_PREFIX, dtype=jnp.int32))

    def one_sample(sample_q, prompt_cache, length):
        key_rows = prompt_cache[0].reshape(CONTINUE_MAX, KEY_VALUE_HEADS, HEAD_SIZE)
        value_rows = prompt_cache[1].reshape(CONTINUE_MAX, KEY_VALUE_HEADS, HEAD_SIZE)
        valid = (jnp.arange(CONTINUE_MAX, dtype=jnp.int32) < length)[None, None, None, :]
        out, top, total = attend_block(sample_q[None], key_rows, value_rows, valid, scale)
        return (out[0], top[0], total[0])
    suffix_out, suffix_top, suffix_total = jax.vmap(one_sample)(query_rows, sample_key_value_cache, suffix_len)
    tops = jnp.concatenate([block_top, suffix_top[None]], axis=0)
    outs = jnp.concatenate([block_out, suffix_out[None]], axis=0)
    totals = jnp.concatenate([block_total, suffix_total[None]], axis=0)
    top = lax.optimization_barrier(jnp.max(tops, axis=0))
    factor = jnp.exp(tops - top[None])
    numer = lax.optimization_barrier(jnp.sum(outs * factor[..., None], axis=0))
    denom = lax.optimization_barrier(jnp.sum(totals * factor, axis=0))
    attention = (numer / denom[..., None]).astype(jnp.bfloat16).reshape(SAMPLE_COUNT, QUERY_HEADS * HEAD_SIZE)
    return jnp.dot(attention, w_out, preferred_element_type=jnp.float32).astype(jnp.bfloat16)
```

```python
import math, functools
import jax, jax.numpy as jnp
from jax import lax
from jax.experimental import pallas as pl
from jax.experimental.pallas import tpu as pltpu
from jax.sharding import PartitionSpec as P

LOG2E = 1.4426950408889634

def prep_kernel(n_ref, sc_ref, code_ref, k_ref, v_ref, x_s, k0_s, *, tb, sb):
    i = pl.program_id(0)
    heads = code_ref.shape[2]
    lanes = code_ref.shape[3]
    n = n_ref[0]
    row = lax.broadcasted_iota(jnp.int32, (sb, lanes), 0)
    for b in range(tb // sb):
        t0 = i * tb + b * sb
        ok = row < n - t0
        blk = i * (tb // sb) + b
        for c in range(2):
            x = code_ref[c, b * sb:(b + 1) * sb].astype(jnp.float32)
            x_s[c] = x.reshape(sb * heads, lanes)
            for j in range(heads):
                y = x_s[c, pl.ds(j, sb, stride=heads), :]
                y = y * sc_ref[c, blk * heads + j]
                if c == 0:
                    if b == 0:
                        @pl.when(i == 0)
                        def _():
                            k0_s[j] = jnp.broadcast_to(y[0:1], (8, lanes))
                    y = jnp.where(ok, y, k0_s[j, 0:1])
                    k_ref[j, b * sb:(b + 1) * sb, :] = y.astype(jnp.bfloat16)
                else:
                    y = jnp.where(ok, y, 0.0)
                    v_ref[j, b * sb:(b + 1) * sb, 0:lanes] = y.astype(jnp.bfloat16)
                    v_ref[j, b * sb:(b + 1) * sb, lanes:2 * lanes] = jnp.where(ok, 1.0, 0.0).astype(jnp.bfloat16)

def prep(n, scale, code, tb=256):
    _, T, H, D = code.shape
    sb = T // scale.shape[1]
    sc = scale.astype(jnp.float32).reshape(2, -1)
    return pl.pallas_call(
        functools.partial(prep_kernel, tb=tb, sb=sb),
        grid=(T // tb,),
        in_specs=[pl.BlockSpec(memory_space=pltpu.SMEM), pl.BlockSpec(memory_space=pltpu.SMEM),
                  pl.BlockSpec((2, tb, H, D), lambda i: (0, i, 0, 0))],
        out_specs=[pl.BlockSpec((H, tb, D), lambda i: (0, i, 0)), pl.BlockSpec((H, tb, 2 * D), lambda i: (0, i, 0))],
        out_shape=[jax.ShapeDtypeStruct((H, T, D), jnp.bfloat16), jax.ShapeDtypeStruct((H, T, 2 * D), jnp.bfloat16)],
        scratch_shapes=[pltpu.VMEM((2, sb * H, D), jnp.float32), pltpu.VMEM((H, 8, D), jnp.float32)],
        compiler_params=pltpu.CompilerParams(vmem_limit_bytes=40 << 20),
        cost_estimate=pl.CostEstimate(flops=16 << 20, bytes_accessed=20 << 20, transcendentals=0),
        name="prep",
    )(n, sc, code)

def suffix_kernel(len_ref, q_ref, c_ref, o_ref, m_ref, t_ref, *, cs):
    T = c_ref.shape[2]
    D = q_ref.shape[1]
    H = c_ref.shape[3] // D
    G = q_ref.shape[0] // H
    length = len_ref[0]
    valid = lax.broadcasted_iota(jnp.int32, (G, T), 1) < length
    q = q_ref[...].astype(jnp.float32)
    for j in range(H):
        qj = q[j * G:(j + 1) * G].astype(jnp.bfloat16)
        s = lax.dot_general(qj, c_ref[0, 0, :, j * D:(j + 1) * D], (((1,), (1,)), ((), ())), preferred_element_type=jnp.float32) * cs
        s = jnp.where(valid, s, -jnp.inf)
        m = jnp.max(s, axis=1, keepdims=True)
        w = jnp.exp2(s - m).astype(jnp.bfloat16)
        t = jnp.sum(w.astype(jnp.float32), axis=1, keepdims=True)
        o = jnp.dot(w, c_ref[0, 1, :, j * D:(j + 1) * D], preferred_element_type=jnp.float32)
        o_ref[j * G:(j + 1) * G, :] = o
        m_ref[j * G:(j + 1) * G, :] = jnp.broadcast_to(m, (G, D))
        t_ref[j * G:(j + 1) * G, :] = jnp.broadcast_to(t, (G, D))

def suffix(length, q, cache):
    HQ, D = q.shape
    return pl.pallas_call(
        functools.partial(suffix_kernel, cs=LOG2E / math.sqrt(D)),
        in_specs=[pl.BlockSpec(memory_space=pltpu.SMEM), pl.BlockSpec(memory_space=pltpu.VMEM), pl.BlockSpec(memory_space=pltpu.VMEM)],
        out_specs=[pl.BlockSpec(memory_space=pltpu.VMEM)] * 3,
        out_shape=[jax.ShapeDtypeStruct((HQ, D), jnp.float32)] * 3,
        compiler_params=pltpu.CompilerParams(vmem_limit_bytes=40 << 20),
        cost_estimate=pl.CostEstimate(flops=1 << 27, bytes_accessed=2 << 20, transcendentals=0),
        name="suffix",
    )(length, q, cache)

def attn_kernel(meta_ref, qg_ref, k_ref, v_ref, so_ref, sm_ref, st_ref, out_ref, q_s, *, cs, rows, k_heads):
    j = pl.program_id(0)
    S, HQ, D = qg_ref.shape
    H = pl.num_programs(0)
    G = HQ // k_heads
    n = meta_ref[0]
    me = meta_ref[1]
    @pl.when(j == 0)
    def _():
        q_s[...] = qg_ref[...].astype(jnp.float32).reshape(S * HQ, D)
    R = G * S
    hp = 64 // S
    sidx = lax.broadcasted_iota(jnp.int32, (S, D), 0)
    neg = -(2.0 ** 127)
    for r in range(R // rows):
        hs = rows // S
        q = jnp.concatenate([q_s[pl.ds(j * G + r * hs + h, S, stride=HQ), :] for h in range(hs)], axis=0).astype(jnp.bfloat16)
        z = lax.dot_general(q, k_ref[0], (((1,), (1,)), ((), ())), preferred_element_type=jnp.float32)
        m = jnp.max(z, axis=1, keepdims=True) * cs
        m = jnp.broadcast_to(m, (rows, D))
        m = m.astype(jnp.bfloat16).astype(jnp.float32)
        p = jnp.exp2(z * cs - m[:, 0:1]).astype(jnp.bfloat16)
        o = jnp.dot(p, v_ref[0], preferred_element_type=jnp.float32)
        tot = o[:, D:]
        o = o[:, :D]
        m = jnp.where(n > 0, m, neg)
        mts = []
        for h in range(hs):
            hh = r * hs + h
            sl = slice(h * S, (h + 1) * S)
            so = so_ref[pl.ds(j * G + hh, 1), :]
            sm = sm_ref[pl.ds(j * G + hh, 1), :]
            st = st_ref[pl.ds(j * G + hh, 1), :]
            mine = sidx == me
            sm2 = jnp.where(mine, sm, neg)
            mn = jnp.maximum(m[sl], sm2).astype(jnp.bfloat16).astype(jnp.float32)
            fa = jnp.exp2(m[sl] - mn)
            fb = jnp.where(mine, jnp.exp2(sm2 - mn), 0.0)
            on = o[sl] * fa + so * fb
            tn = tot[sl] * fa + st * fb
            d, hd = divmod(hh, hp)
            out_ref[d, hd * S:(hd + 1) * S, :] = on.astype(jnp.bfloat16)
            mts.append((mn, tn))
        for d0 in range(hs // hp):
            mm = jnp.concatenate([a for a, _ in mts[d0 * hp:(d0 + 1) * hp]], axis=0)
            tt = jnp.concatenate([b for _, b in mts[d0 * hp:(d0 + 1) * hp]], axis=0)
            diag = lax.broadcasted_iota(jnp.int32, (64, D), 0) == lax.broadcasted_iota(jnp.int32, (64, D), 1)
            mr = jnp.sum(jnp.where(diag, mm, 0.0), axis=0, keepdims=True)
            tr = jnp.sum(jnp.where(diag, tt, 0.0), axis=0, keepdims=True)
            hi = tr.astype(jnp.bfloat16).astype(jnp.float32)
            lo = tr - hi
            st = jnp.concatenate([mr, hi, lo, jnp.zeros((13, D), jnp.float32)], axis=0)
            out_ref[(r * hs) // hp + d0, 64:80, :] = st.astype(jnp.bfloat16)

def attn(meta, qg, k, v, so, sm, st, rows=256):
    S, HQ, D = qg.shape
    H, T, _ = k.shape
    nd = HQ * S // 64
    whole = lambda shape: pl.BlockSpec(shape, lambda j: (0,) * len(shape))
    return pl.pallas_call(
        functools.partial(attn_kernel, cs=LOG2E / math.sqrt(D), rows=rows, k_heads=H),
        grid=(H,),
        in_specs=[pl.BlockSpec(memory_space=pltpu.SMEM), whole(qg.shape),
                  pl.BlockSpec((1, T, D), lambda j: (j, 0, 0)), pl.BlockSpec((1, T, 2 * D), lambda j: (j, 0, 0)),
                  whole(so.shape), whole(sm.shape), whole(st.shape)],
        out_specs=pl.BlockSpec((nd // H, 80, D), lambda j: (j, 0, 0)),
        out_shape=jax.ShapeDtypeStruct((nd, 80, D), jnp.bfloat16),
        scratch_shapes=[pltpu.VMEM((S * HQ, D), jnp.float32)],
        compiler_params=pltpu.CompilerParams(vmem_limit_bytes=48 << 20),
        cost_estimate=pl.CostEstimate(flops=2 << 30, bytes_accessed=12 << 20, transcendentals=4 << 20),
        name="attn",
    )(meta, qg, k, v, so, sm, st)

def combine_kernel(r_ref, o_ref, st_s):
    B = r_ref.shape[0]
    D = r_ref.shape[2]
    st_s[...] = r_ref[:, 64:80, :].astype(jnp.float32).reshape(B * 16, D)
    m = st_s[pl.ds(0, B, stride=16), :]
    t = st_s[pl.ds(1, B, stride=16), :] + st_s[pl.ds(2, B, stride=16), :]
    M = jnp.max(m, axis=0, keepdims=True)
    f = jnp.exp2(m - M)
    den = jnp.sum(f * t, axis=0, keepdims=True)
    lane = lax.broadcasted_iota(jnp.int32, (B, D), 1)
    f = jnp.where(lane < 64, f / den, 0.0)
    ft = jnp.transpose(jnp.concatenate([f, jnp.zeros((D - B, D), jnp.float32)], axis=0))[:64]
    acc = jnp.zeros((64, D), jnp.float32)
    for b in range(B):
        acc = acc + r_ref[b, 0:64, :].astype(jnp.float32) * ft[:, b:b + 1]
    res = jnp.concatenate([acc[:32], acc[32:]], axis=1).astype(jnp.bfloat16)
    for g in range(o_ref.shape[0]):
        o_ref[g] = res

def combine(r, copies):
    B, _, D = r.shape
    return pl.pallas_call(
        combine_kernel,
        in_specs=[pl.BlockSpec(memory_space=pltpu.VMEM)],
        out_specs=pl.BlockSpec(memory_space=pltpu.VMEM),
        out_shape=jax.ShapeDtypeStruct((copies, 32, 2 * D), jnp.bfloat16),
        scratch_shapes=[pltpu.VMEM((B * 16, D), jnp.float32)],
        compiler_params=pltpu.CompilerParams(vmem_limit_bytes=40 << 20),
        cost_estimate=pl.CostEstimate(flops=1 << 20, bytes_accessed=1 << 20, transcendentals=0),
        name="combine",
    )(r)

def body(query, prompt_code_cache, prompt_scale_cache, prefix_len, sample_key_value_cache, suffix_len, w_out):
    chunk = prompt_code_cache.shape[1]
    head_width = prompt_code_cache.shape[3]
    heads = query.shape[1] // head_width
    members = lax.axis_size("prefix")
    groups = lax.axis_size("samples")
    me = lax.axis_index("prefix").astype(jnp.int32)
    valid = jnp.clip(prefix_len - me * chunk, 0, chunk)

    def swap(x, axis):
        return lax.all_to_all(x, axis, split_axis=0, concat_axis=0, tiled=True)

    own = query.reshape(heads, head_width)
    gathered = swap(jnp.broadcast_to(own[None], (members, heads, head_width)), "prefix")
    keys, values = prep(valid, prompt_scale_cache, prompt_code_cache)
    so, sm, st = suffix(suffix_len, own, sample_key_value_cache)
    meta = jnp.concatenate([valid, me[None]])
    partials = attn(meta, gathered, keys, values, so, sm, st)
    attention = combine(swap(partials, "prefix"), groups)
    rows = swap(attention, "samples").reshape(-1, attention.shape[2])
    terms = jnp.dot(rows, w_out, preferred_element_type=jnp.float32).astype(jnp.bfloat16)
    terms = swap(terms.reshape(members, -1, terms.shape[1]), "prefix")
    return jnp.sum(terms.astype(jnp.float32), axis=0).astype(jnp.bfloat16)


def solution(mesh):
    in_specs = (
        P(("samples", "prefix"), None),
        P(None, "prefix", None, None),
        P(None, "prefix", None),
        P(),
        P(("samples", "prefix"), None, None, None),
        P(("samples", "prefix")),
        P("prefix", "samples"),
    )
    return jax.shard_map(body, mesh=mesh, in_specs=in_specs, out_specs=P("prefix", "samples"), check_vma=False)
```

```python
import math, functools
import jax, jax.numpy as jnp
from jax import lax
from jax.experimental import pallas as pl
from jax.experimental.pallas import tpu as pltpu
from jax.sharding import PartitionSpec as P
LOG2E = 1.4426950408889634
FLOOR = -(2.0 ** 127)

def prep_kernel(n_ref, len_ref, sc_ref, code_hbm, q_ref, cache_hbm, k_hbm, v_hbm, own_ref, code_s, cache_s, k_s, v_s, hot_s, in_sem, cache_sem, k_sem, v_sem, *, tb, sb, cs):
    H, _, lanes = k_s.shape
    G = own_ref.shape[1] // H
    steps = k_s.shape[1] // tb

    def rows(i, size):
        return pl.ds(pl.multiple_of(i * size, size), size)

    def load(i):
        return pltpu.make_async_copy(code_hbm.at[:, rows(i, tb * H), :], code_s.at[:, rows(i, tb * H), :], in_sem.at[i])

    def save(i):
        at = rows(i, tb)
        return (pltpu.make_async_copy(k_s.at[:, at, :], k_hbm.at[:, at, :], k_sem.at[i]),
                pltpu.make_async_copy(v_s.at[:, at, :], v_hbm.at[:, at, :], v_sem.at[i]))

    cache_copy = pltpu.make_async_copy(cache_hbm, cache_s, cache_sem)
    load(0).start()
    cache_copy.start()
    for i in range(1, steps):
        load(i).start()
    hr = hot_s.shape[0]
    half = sb // 2
    r = lax.broadcasted_iota(jnp.int32, (hr, hr), 0)
    c = lax.broadcasted_iota(jnp.int32, (hr, hr), 1)
    hot_s[...] = jnp.where((r % half) * H + r // half == c, 1.0, 0.0).astype(jnp.bfloat16)

    @pl.loop(0, steps)
    def _(i):
        load(i).wait()
        prep_step(i, n_ref, sc_ref, code_s, k_s, v_s, hot_s, tb=tb, sb=sb)
        for copy in save(i):
            copy.start()

    cache_copy.wait()
    q = q_ref[...].astype(jnp.float32)
    for i in range(H):
        own = jnp.concatenate([q[:, h * lanes:(h + 1) * lanes] for h in range(i * G, (i + 1) * G)], axis=0).astype(jnp.bfloat16)
        cols = slice(i * lanes, (i + 1) * lanes)
        grp = slice(i * G, (i + 1) * G)
        T = cache_s.shape[2]
        s = lax.dot_general(own, cache_s[0, 0, :, cols], (((1,), (1,)), ((), ())), preferred_element_type=jnp.float32) * cs
        s = jnp.where(lax.broadcasted_iota(jnp.int32, (G, T), 1) < len_ref[0], s, -jnp.inf)
        m = jnp.max(s, axis=1, keepdims=True)
        w = jnp.exp2(s - m).astype(jnp.bfloat16)
        own_ref[0, grp, :] = jnp.dot(w, cache_s[0, 1, :, cols], preferred_element_type=jnp.float32)
        own_ref[1, grp, :] = jnp.broadcast_to(m, (G, lanes))
        own_ref[2, grp, :] = jnp.broadcast_to(jnp.sum(w.astype(jnp.float32), axis=1, keepdims=True), (G, lanes))
    for i in range(steps):
        for copy in save(i):
            copy.wait()


def prep_step(i, n_ref, sc_ref, code_ref, k_ref, v_ref, hot_s, *, tb, sb):
    heads = k_ref.shape[0]
    lanes = code_ref.shape[2]
    half = sb // 2
    hr = half * heads
    n = n_ref[0]

    def move(c, b):
        x = jnp.concatenate([code_ref[c, pl.ds(pl.multiple_of(i * tb * heads, tb * heads) + (2 * b + u) * hr, hr), :] for u in range(2)], axis=1)
        y = jnp.dot(hot_s[...], x, preferred_element_type=jnp.float32)
        blk = i * (tb // sb) + b
        return [y[j * half:(j + 1) * half] * sc_ref[c, blk * heads + j] for j in range(heads)]

    def go(masked):
        for b in range(tb // sb):
            rows = [pl.ds(pl.multiple_of(i * tb, tb) + b * sb + u * half, half) for u in range(2)]
            if masked:
                left = n - i * tb - b * sb
                ok = [lax.broadcasted_iota(jnp.int32, (half, lanes), 0) + u * half < left for u in range(2)]
            for c in range(2):
                ys = move(c, b)
                if masked and c == 0 and b == 0:
                    first = [y[0:1, 0:lanes] for y in ys]
                for j in range(heads):
                    for u in range(2):
                        y = ys[j][:, u * lanes:(u + 1) * lanes]
                        if c == 0:
                            if masked:
                                y = jnp.where(ok[u], y, first[j])
                            k_ref[j, rows[u], :] = y.astype(jnp.bfloat16)
                        else:
                            if masked:
                                y = jnp.where(ok[u], y, 0.0)
                            v_ref[j, rows[u], :] = y.astype(jnp.bfloat16)

    whole = (i + 1) * tb <= n
    some = i * tb < n

    @pl.when(whole)
    def _():
        go(False)

    @pl.when(jnp.logical_and(some, jnp.logical_not(whole)))
    def _():
        go(True)

    @pl.when(jnp.logical_not(some))
    def _():
        for j in range(heads):
            k_ref[j, pl.ds(pl.multiple_of(i * tb, tb), tb), :] = jnp.broadcast_to(jnp.where(i == 0, 0.0, k_ref[j, 0:16].astype(jnp.float32)[0:1]), (tb, lanes)).astype(jnp.bfloat16)
            v_ref[j, pl.ds(pl.multiple_of(i * tb, tb), tb), :] = jnp.zeros((tb, lanes), jnp.bfloat16)

def prep(n, length, scale, code, q, cache):
    _, T, H, D = code.shape
    tb = T // 4
    sb = T // scale.shape[1]
    G = q.shape[1] // (H * D)
    sc = scale.astype(jnp.float32).reshape(2, -1)
    smem = pl.BlockSpec(memory_space=pltpu.SMEM)
    vmem = pl.BlockSpec(memory_space=pltpu.VMEM)
    hbm = pl.BlockSpec(memory_space=pltpu.HBM)
    return pl.pallas_call(
        functools.partial(prep_kernel, tb=tb, sb=sb, cs=LOG2E / math.sqrt(D)),
        in_specs=[smem, smem, smem, hbm, vmem, hbm],
        out_specs=[hbm, hbm, vmem],
        out_shape=[jax.ShapeDtypeStruct((H, T, D), jnp.bfloat16)] * 2 + [jax.ShapeDtypeStruct((3, H * G, D), jnp.float32)],
        scratch_shapes=[pltpu.VMEM((2, T * H, D), jnp.bfloat16), pltpu.VMEM(cache.shape, jnp.bfloat16),
                        pltpu.VMEM((H, T, D), jnp.bfloat16), pltpu.VMEM((H, T, D), jnp.bfloat16),
                        pltpu.VMEM((sb // 2 * H, sb // 2 * H), jnp.bfloat16),
                        pltpu.SemaphoreType.DMA((T // tb,)), pltpu.SemaphoreType.DMA,
                        pltpu.SemaphoreType.DMA((T // tb,)), pltpu.SemaphoreType.DMA((T // tb,))],
        compiler_params=pltpu.CompilerParams(vmem_limit_bytes=63_300_000),
        cost_estimate=pl.CostEstimate(flops=16 << 20, bytes_accessed=20 << 20, transcendentals=0),
        name="prep",
    )(n, length, sc, code.reshape(2, T * H, D), q, cache)

def attn_kernel(n_ref, me_ref, qg_hbm, k_hbm, v_hbm, own_hbm, out_ref, qg_ref, own_ref, qg_sem, own_sem, q_s, k_ref, v_ref, one_s, k_sem, v_sem, *s_s, cs, tile, nbuf):
    S, HQ, D = qg_ref.shape
    H, T, _ = k_hbm.shape
    G = HQ // H
    n = n_ref[0]
    me = me_ref[0]
    R = G * S
    hp = 64 // S
    load_k = [pltpu.make_async_copy(k_hbm.at[j], k_ref.at[j], k_sem.at[j]) for j in range(H)]
    load_v = [pltpu.make_async_copy(v_hbm.at[j], v_ref.at[j], v_sem.at[j]) for j in range(H)]
    load_own = pltpu.make_async_copy(own_hbm, own_ref, own_sem)
    load_q = pltpu.make_async_copy(qg_hbm, qg_ref, qg_sem)
    load_q.start()
    load_k[0].start()
    load_k[1].start()
    load_v[0].start()
    load_own.start()
    one_s[...] = jnp.where(lax.broadcasted_iota(jnp.int32, (T, D), 0) < n, 1.0, 0.0).astype(jnp.bfloat16)
    sidx = lax.broadcasted_iota(jnp.int32, (S, D), 0)
    load_q.wait()
    q_s[...] = qg_ref[...].astype(jnp.float32).reshape(S * HQ, D)
    ms = {}
    def scores(j, c):
        if c == 0:
            q = jnp.concatenate([q_s[pl.ds(j * G + h, S, stride=HQ), :] for h in range(G)], axis=0).astype(jnp.bfloat16)
            ms[j] = [q, None]
        q = ms[j][0]
        z = lax.dot_general(q, k_ref[j, c * tile:(c + 1) * tile, :], (((1,), (1,)), ((), ())), preferred_element_type=jnp.float32)
        s_s[j % nbuf][:, c * tile:(c + 1) * tile] = z
        m = ms[j][1]
        for l in range(tile // D):
            zz = z[:, l * D:(l + 1) * D]
            m = zz if m is None else jnp.maximum(m, zz)
        ms[j][1] = m
        if (c + 1) * tile == T:
            m = jnp.max(m, axis=1, keepdims=True) * cs
            ms[j][1] = jnp.broadcast_to(m, (R, D)).astype(jnp.bfloat16).astype(jnp.float32)
    acc = {}
    def weigh(j, c):
        m = ms[j][1]
        z = s_s[j % nbuf][:, c * tile:(c + 1) * tile]
        p = jnp.exp2(z * cs - jnp.concatenate([m] * (tile // D), axis=1)).astype(jnp.bfloat16)
        at = slice(c * tile, (c + 1) * tile)
        o = jnp.dot(p, jnp.concatenate([v_ref[j, at, :], one_s[at, :]], axis=1), preferred_element_type=jnp.float32)
        acc[j] = o if c == 0 else acc[j] + o
    def finish(j):
        o = acc[j][:, :D]
        tot = acc[j][:, D:]
        m = jnp.where(n > 0, ms[j][1], FLOOR)
        mts = []
        for h in range(G):
            sl = slice(h * S, (h + 1) * S)
            r = j * G + h
            mine = sidx == me
            sm2 = jnp.where(mine, own_ref[1, r:r + 1, :], FLOOR)
            mn = jnp.maximum(m[sl], sm2).astype(jnp.bfloat16).astype(jnp.float32)
            fa = jnp.exp2(m[sl] - mn)
            fb = jnp.where(mine, jnp.exp2(sm2 - mn), 0.0)
            on = o[sl] * fa + own_ref[0, r:r + 1, :] * fb
            tn = tot[sl] * fa + own_ref[2, r:r + 1, :] * fb
            d, hd = divmod(r, hp)
            out_ref[d, hd * S:(hd + 1) * S, :] = on.astype(jnp.bfloat16)
            mts.append((mn, tn))
        diag = lax.broadcasted_iota(jnp.int32, (64, D), 0) == lax.broadcasted_iota(jnp.int32, (64, D), 1)
        for d0 in range(G // hp):
            mm = jnp.concatenate([a for a, _ in mts[d0 * hp:(d0 + 1) * hp]], axis=0)
            tt = jnp.concatenate([b for _, b in mts[d0 * hp:(d0 + 1) * hp]], axis=0)
            mr = jnp.sum(jnp.where(diag, mm, 0.0), axis=0, keepdims=True)
            tr = jnp.sum(jnp.where(diag, tt, 0.0), axis=0, keepdims=True)
            hi = tr.astype(jnp.bfloat16).astype(jnp.float32)
            st = jnp.concatenate([mr, hi, tr - hi, jnp.zeros((13, D), jnp.float32)], axis=0)
            out_ref[j * (G // hp) + d0, 64:80, :] = st.astype(jnp.bfloat16)
    nt = T // tile
    K = lambda *a: [('k', i) for i in a]
    V = lambda *a: [('v', i) for i in a]
    waits = {0: K(0), 1: K(1) + V(0), 2: K(2, 3) + V(1, 2), 4: K(4, 5) + V(3, 4), 6: K(6, 7) + V(5, 6, 7)}
    plan = {0: K(2, 3) + V(1, 2), 1: K(4, 5) + V(3, 4), 3: K(6, 7) + V(5, 6, 7)}
    for j in range(H + 1):
        for c in range(nt):
            if j < H:
                if c == 0:
                    if j == 1:
                        load_own.wait()
                    for which, i in waits.get(j, ()):
                        (load_k if which == 'k' else load_v)[i].wait()
                    for which, i in plan.get(j, ()):
                        (load_k if which == 'k' else load_v)[i].start()
                scores(j, c)
            if j == H and c == 0:
                for which, i in waits.get(j, ()):
                    (load_k if which == 'k' else load_v)[i].wait()
            if j > 0:
                weigh(j - 1, c)
        if j > 0:
            finish(j - 1)

def attn(n, me, qg, k, v, own, tile=256, nbuf=2):
    S, HQ, D = qg.shape
    H, T, _ = k.shape
    nd = HQ * S // 64
    vm = pl.BlockSpec(memory_space=pltpu.VMEM)
    hbm = pl.BlockSpec(memory_space=pltpu.HBM)
    return pl.pallas_call(
        functools.partial(attn_kernel, cs=LOG2E / math.sqrt(D), tile=tile, nbuf=nbuf),
        in_specs=[pl.BlockSpec(memory_space=pltpu.SMEM)] * 2 + [hbm] * 4,
        out_specs=vm,
        out_shape=jax.ShapeDtypeStruct((nd, 80, D), jnp.bfloat16),
        scratch_shapes=[pltpu.VMEM(qg.shape, qg.dtype), pltpu.VMEM(own.shape, own.dtype), pltpu.SemaphoreType.DMA, pltpu.SemaphoreType.DMA, pltpu.VMEM((S * HQ, D), jnp.float32), pltpu.VMEM((H, T, D), jnp.bfloat16), pltpu.VMEM((H, T, D), jnp.bfloat16), pltpu.VMEM((T, D), jnp.bfloat16),
                        pltpu.SemaphoreType.DMA((H,)), pltpu.SemaphoreType.DMA((H,))] + [pltpu.VMEM((S * HQ // H, T), jnp.float32)] * nbuf,
        compiler_params=pltpu.CompilerParams(vmem_limit_bytes=63_300_000),
        cost_estimate=pl.CostEstimate(flops=2 << 30, bytes_accessed=12 << 20, transcendentals=4 << 20),
        name="attn",
    )(n, me, qg, k, v, own)

def combine_kernel(r_ref, o_ref, st_s):
    B = r_ref.shape[0]
    D = r_ref.shape[2]
    st_s[...] = r_ref[:, 64:80, :].astype(jnp.float32).reshape(B * 16, D)
    m = st_s[pl.ds(0, B, stride=16), :]
    t = st_s[pl.ds(1, B, stride=16), :] + st_s[pl.ds(2, B, stride=16), :]
    M = jnp.max(m, axis=0, keepdims=True)
    f = jnp.exp2(m - M)
    den = jnp.sum(f * t, axis=0, keepdims=True)
    lane = lax.broadcasted_iota(jnp.int32, (B, D), 1)
    f = jnp.where(lane < 64, f / den, 0.0)
    ft = jnp.transpose(jnp.concatenate([f, jnp.zeros((D - B, D), jnp.float32)], axis=0))[:64]
    acc = jnp.zeros((64, D), jnp.float32)
    for b in range(B):
        acc = acc + r_ref[b, 0:64, :].astype(jnp.float32) * ft[:, b:b + 1]
    res = jnp.concatenate([acc[:32], acc[32:]], axis=1).astype(jnp.bfloat16)
    for g in range(o_ref.shape[0]):
        o_ref[g] = res

def combine(r, copies):
    B, _, D = r.shape
    return pl.pallas_call(
        combine_kernel,
        in_specs=[pl.BlockSpec(memory_space=pltpu.VMEM)],
        out_specs=pl.BlockSpec(memory_space=pltpu.VMEM),
        out_shape=jax.ShapeDtypeStruct((copies, 32, 2 * D), jnp.bfloat16),
        scratch_shapes=[pltpu.VMEM((B * 16, D), jnp.float32)],
        compiler_params=pltpu.CompilerParams(vmem_limit_bytes=10 << 20),
        cost_estimate=pl.CostEstimate(flops=1 << 20, bytes_accessed=1 << 20, transcendentals=0),
        name="combine",
    )(r)

def spread_kernel(q_ref, o_ref):
    M, HQ, D = o_ref.shape
    q = q_ref[...].astype(jnp.float32)
    x = jnp.concatenate([q[:, h * D:(h + 1) * D] for h in range(HQ)], axis=0).astype(jnp.bfloat16)
    for i in range(M):
        o_ref[i] = x

def spread(q, members, width):
    vm = pl.BlockSpec(memory_space=pltpu.VMEM)
    return pl.pallas_call(
        spread_kernel, in_specs=[vm], out_specs=vm,
        out_shape=jax.ShapeDtypeStruct((members, q.shape[1] // width, width), q.dtype),
        compiler_params=pltpu.CompilerParams(vmem_limit_bytes=10 << 20),
        cost_estimate=pl.CostEstimate(flops=1 << 18, bytes_accessed=1 << 19, transcendentals=0),
        name="spread",
    )(q)

def body(query, prompt_code_cache, prompt_scale_cache, prefix_len, sample_key_value_cache, suffix_len, w_out):
    chunk = prompt_code_cache.shape[1]
    head_width = prompt_code_cache.shape[3]
    members = lax.axis_size("prefix")
    groups = lax.axis_size("samples")
    me = lax.axis_index("prefix").astype(jnp.int32)
    valid = jnp.clip(prefix_len - me * chunk, 0, chunk)

    def swap(x, axis):
        return lax.all_to_all(x, axis, split_axis=0, concat_axis=0, tiled=True)

    gathered = swap(spread(query, members, head_width), "prefix")
    keys, values, own = prep(valid, suffix_len, prompt_scale_cache, prompt_code_cache, query, sample_key_value_cache)
    partials = attn(valid, me[None], gathered, keys, values, own)
    attention = combine(swap(partials, "prefix"), groups)
    rows = swap(attention, "samples").reshape(-1, attention.shape[2])
    terms = jnp.dot(rows, w_out, preferred_element_type=jnp.float32).astype(jnp.bfloat16)
    terms = swap(terms.reshape(members, -1, terms.shape[1]), "prefix")
    return jnp.sum(terms.astype(jnp.float32), axis=0).astype(jnp.bfloat16)


def solution(mesh):
    in_specs = (
        P(("samples", "prefix"), None),
        P(None, "prefix", None, None),
        P(None, "prefix", None),
        P(),
        P(("samples", "prefix"), None, None, None),
        P(("samples", "prefix")),
        P("prefix", "samples"),
    )
    return jax.shard_map(body, mesh=mesh, in_specs=in_specs, out_specs=P("prefix", "samples"), check_vma=False)
```

```python
import math, functools
import jax, jax.numpy as jnp
from jax import lax
from jax.experimental import pallas as pl
from jax.experimental.pallas import tpu as pltpu
from jax.sharding import PartitionSpec as P
LOG2E = 1.4426950408889634
FLOOR = -(2.0 ** 127)

def valid_rows(plen_ref, chunk):
    return jnp.clip(plen_ref[0] - lax.axis_index("prefix") * chunk, 0, chunk)

def prep_kernel(plen_ref, len_ref, scale_ref, code_hbm, q_ref, cache_hbm, k_hbm, v_hbm, own_ref, code_s, cache_s, k_s, v_s, hot_s, sc_v, sc_ref, sc_sem, in_sem, cache_sem, k_sem, v_sem, *, tb, sb, cs):
    H, T, lanes = k_s.shape
    G = own_ref.shape[1] // H
    steps = k_s.shape[1] // tb

    def rows(i, size):
        return pl.ds(pl.multiple_of(i * size, size), size)

    def load(i):
        return pltpu.make_async_copy(code_hbm.at[:, rows(i, tb * H), :], code_s.at[:, rows(i, tb * H), :], in_sem.at[i])

    def save(i):
        at = rows(i, tb)
        return (pltpu.make_async_copy(k_s.at[:, at, :], k_hbm.at[:, at, :], k_sem.at[i]),
                pltpu.make_async_copy(v_s.at[:, at, :], v_hbm.at[:, at, :], v_sem.at[i]))

    cache_copy = pltpu.make_async_copy(cache_hbm, cache_s, cache_sem)
    load(0).start()
    cache_copy.start()
    for i in range(1, steps):
        load(i).start()
    B = scale_ref.shape[2]
    for c in range(2):
        sc_v[c * H:(c + 1) * H, 0:B] = scale_ref[c].astype(jnp.float32)
    sc_copy = pltpu.make_async_copy(sc_v, sc_ref, sc_sem)
    sc_copy.start()
    n = valid_rows(plen_ref, T)
    hr = hot_s.shape[0]
    half = sb // 2
    r = lax.broadcasted_iota(jnp.int32, (hr, hr), 0)
    c = lax.broadcasted_iota(jnp.int32, (hr, hr), 1)
    hot_s[...] = jnp.where((r % half) * H + r // half == c, 1.0, 0.0).astype(jnp.bfloat16)

    sc_copy.wait()

    @pl.loop(0, steps)
    def _(i):
        load(i).wait()
        prep_step(i, n, sc_ref, code_s, k_s, v_s, hot_s, tb=tb, sb=sb)
        for copy in save(i):
            copy.start()

    cache_copy.wait()
    q = q_ref[...].astype(jnp.float32)
    for i in range(H):
        own = jnp.concatenate([q[:, h * lanes:(h + 1) * lanes] for h in range(i * G, (i + 1) * G)], axis=0).astype(jnp.bfloat16)
        cols = slice(i * lanes, (i + 1) * lanes)
        grp = slice(i * G, (i + 1) * G)
        C = cache_s.shape[2]
        s = lax.dot_general(own, cache_s[0, 0, :, cols], (((1,), (1,)), ((), ())), preferred_element_type=jnp.float32) * cs
        s = jnp.where(lax.broadcasted_iota(jnp.int32, (G, C), 1) < len_ref[0], s, -jnp.inf)
        m = jnp.max(s, axis=1, keepdims=True)
        w = jnp.exp2(s - m).astype(jnp.bfloat16)
        own_ref[0, grp, :] = jnp.dot(w, cache_s[0, 1, :, cols], preferred_element_type=jnp.float32)
        own_ref[1, grp, :] = jnp.broadcast_to(m, (G, lanes))
        own_ref[2, grp, :] = jnp.broadcast_to(jnp.sum(w.astype(jnp.float32), axis=1, keepdims=True), (G, lanes))
    for i in range(steps):
        for copy in save(i):
            copy.wait()


def prep_step(i, n, sc_ref, code_ref, k_ref, v_ref, hot_s, *, tb, sb):
    heads = k_ref.shape[0]
    lanes = code_ref.shape[2]
    half = sb // 2
    hr = half * heads

    def move(c, b):
        x = jnp.concatenate([code_ref[c, pl.ds(pl.multiple_of(i * tb * heads, tb * heads) + (2 * b + u) * hr, hr), :] for u in range(2)], axis=1)
        y = jnp.dot(hot_s[...], x, preferred_element_type=jnp.float32)
        blk = i * (tb // sb) + b
        return [y[j * half:(j + 1) * half] * sc_ref[c * heads + j, blk] for j in range(heads)]

    def go(masked):
        for b in range(tb // sb):
            rows = [pl.ds(pl.multiple_of(i * tb, tb) + b * sb + u * half, half) for u in range(2)]
            if masked:
                left = n - i * tb - b * sb
                ok = [lax.broadcasted_iota(jnp.int32, (half, lanes), 0) + u * half < left for u in range(2)]
            for c in range(2):
                ys = move(c, b)
                if masked and c == 0 and b == 0:
                    first = [y[0:1, 0:lanes] for y in ys]
                for j in range(heads):
                    for u in range(2):
                        y = ys[j][:, u * lanes:(u + 1) * lanes]
                        if c == 0:
                            if masked:
                                y = jnp.where(ok[u], y, first[j])
                            k_ref[j, rows[u], :] = y.astype(jnp.bfloat16)
                        else:
                            if masked:
                                y = jnp.where(ok[u], y, 0.0)
                            v_ref[j, rows[u], :] = y.astype(jnp.bfloat16)

    whole = (i + 1) * tb <= n
    some = i * tb < n

    @pl.when(whole)
    def _():
        go(False)

    @pl.when(jnp.logical_and(some, jnp.logical_not(whole)))
    def _():
        go(True)

    @pl.when(jnp.logical_not(some))
    def _():
        for j in range(heads):
            k_ref[j, pl.ds(pl.multiple_of(i * tb, tb), tb), :] = jnp.broadcast_to(jnp.where(i == 0, 0.0, k_ref[j, 0:16].astype(jnp.float32)[0:1]), (tb, lanes)).astype(jnp.bfloat16)
            v_ref[j, pl.ds(pl.multiple_of(i * tb, tb), tb), :] = jnp.zeros((tb, lanes), jnp.bfloat16)

def prep(n, length, scale, code, q, cache):
    _, T, H, D = code.shape
    tb = T // 8
    sb = T // scale.shape[1]
    G = q.shape[1] // (H * D)
    smem = pl.BlockSpec(memory_space=pltpu.SMEM)
    vmem = pl.BlockSpec(memory_space=pltpu.VMEM)
    hbm = pl.BlockSpec(memory_space=pltpu.HBM)
    return pl.pallas_call(
        functools.partial(prep_kernel, tb=tb, sb=sb, cs=LOG2E / math.sqrt(D)),
        in_specs=[smem, smem, vmem, hbm, vmem, hbm],
        out_specs=[hbm, hbm, vmem],
        out_shape=[jax.ShapeDtypeStruct((H, T, D), jnp.bfloat16)] * 2 + [jax.ShapeDtypeStruct((3, H * G, D), jnp.float32)],
        scratch_shapes=[pltpu.VMEM((2, T * H, D), jnp.bfloat16), pltpu.VMEM(cache.shape, jnp.bfloat16),
                        pltpu.VMEM((H, T, D), jnp.bfloat16), pltpu.VMEM((H, T, D), jnp.bfloat16),
                        pltpu.VMEM((sb // 2 * H, sb // 2 * H), jnp.bfloat16),
                        pltpu.VMEM((2 * H, 128), jnp.float32), pltpu.SMEM((2 * H, 128), jnp.float32), pltpu.SemaphoreType.DMA,
                        pltpu.SemaphoreType.DMA((T // tb,)), pltpu.SemaphoreType.DMA,
                        pltpu.SemaphoreType.DMA((T // tb,)), pltpu.SemaphoreType.DMA((T // tb,))],
        compiler_params=pltpu.CompilerParams(vmem_limit_bytes=63_300_000),
        cost_estimate=pl.CostEstimate(flops=16 << 20, bytes_accessed=20 << 20, transcendentals=0),
        name="prep",
    )(n, length, scale.transpose(0, 2, 1), code.reshape(2, T * H, D), q, cache)

def attn_kernel(plen_ref, qg_hbm, k_hbm, v_hbm, own_hbm, out_ref, qg_ref, own_ref, qg_sem, own_sem, q_s, k_ref, v_ref, one_s, k_sem, v_sem, *s_s, cs, tile, nbuf):
    S, HQ, D = qg_ref.shape
    H, T, _ = k_hbm.shape
    G = HQ // H
    n = valid_rows(plen_ref, T)
    me = lax.axis_index("prefix")
    R = G * S
    hp = 64 // S
    load_k = [pltpu.make_async_copy(k_hbm.at[j], k_ref.at[j], k_sem.at[j]) for j in range(H)]
    load_v = [pltpu.make_async_copy(v_hbm.at[j], v_ref.at[j], v_sem.at[j]) for j in range(H)]
    load_own = pltpu.make_async_copy(own_hbm, own_ref, own_sem)
    load_q = pltpu.make_async_copy(qg_hbm, qg_ref, qg_sem)
    load_q.start()
    load_k[0].start()
    load_k[1].start()
    load_v[0].start()
    load_own.start()
    one_s[...] = jnp.where(lax.broadcasted_iota(jnp.int32, (T, D), 0) < n, 1.0, 0.0).astype(jnp.bfloat16)
    sidx = lax.broadcasted_iota(jnp.int32, (S, D), 0)
    load_q.wait()
    q_s[...] = qg_ref[...].astype(jnp.float32).reshape(S * HQ, D)
    ms = {}
    def scores(j, c):
        if c == 0:
            q = jnp.concatenate([q_s[pl.ds(j * G + h, S, stride=HQ), :] for h in range(G)], axis=0).astype(jnp.bfloat16)
            ms[j] = [q, None]
        q = ms[j][0]
        z = lax.dot_general(q, k_ref[j, c * tile:(c + 1) * tile, :], (((1,), (1,)), ((), ())), preferred_element_type=jnp.float32)
        s_s[j % nbuf][:, c * tile:(c + 1) * tile] = z
        m = ms[j][1]
        for l in range(tile // D):
            zz = z[:, l * D:(l + 1) * D]
            m = zz if m is None else jnp.maximum(m, zz)
        ms[j][1] = m
        if (c + 1) * tile == T:
            m = jnp.max(m, axis=1, keepdims=True) * cs
            ms[j][1] = jnp.broadcast_to(m, (R, D)).astype(jnp.bfloat16).astype(jnp.float32)
    acc = {}
    def weigh(j, c):
        m = ms[j][1]
        z = s_s[j % nbuf][:, c * tile:(c + 1) * tile]
        p = jnp.exp2(z * cs - jnp.concatenate([m] * (tile // D), axis=1)).astype(jnp.bfloat16)
        at = slice(c * tile, (c + 1) * tile)
        o = jnp.dot(p, jnp.concatenate([v_ref[j, at, :], one_s[at, :]], axis=1), preferred_element_type=jnp.float32)
        acc[j] = o if c == 0 else acc[j] + o
    def finish(j):
        o = acc[j][:, :D]
        tot = acc[j][:, D:]
        m = jnp.where(n > 0, ms[j][1], FLOOR)
        mts = []
        for h in range(G):
            sl = slice(h * S, (h + 1) * S)
            r = j * G + h
            mine = sidx == me
            sm2 = jnp.where(mine, own_ref[1, r:r + 1, :], FLOOR)
            mn = jnp.maximum(m[sl], sm2).astype(jnp.bfloat16).astype(jnp.float32)
            fa = jnp.exp2(m[sl] - mn)
            fb = jnp.where(mine, jnp.exp2(sm2 - mn), 0.0)
            on = o[sl] * fa + own_ref[0, r:r + 1, :] * fb
            tn = tot[sl] * fa + own_ref[2, r:r + 1, :] * fb
            d, hd = divmod(r, hp)
            out_ref[d, hd * S:(hd + 1) * S, :] = on.astype(jnp.bfloat16)
            mts.append((mn, tn))
        diag = lax.broadcasted_iota(jnp.int32, (64, D), 0) == lax.broadcasted_iota(jnp.int32, (64, D), 1)
        for d0 in range(G // hp):
            mm = jnp.concatenate([a for a, _ in mts[d0 * hp:(d0 + 1) * hp]], axis=0)
            tt = jnp.concatenate([b for _, b in mts[d0 * hp:(d0 + 1) * hp]], axis=0)
            mr = jnp.sum(jnp.where(diag, mm, 0.0), axis=0, keepdims=True)
            tr = jnp.sum(jnp.where(diag, tt, 0.0), axis=0, keepdims=True)
            hi = tr.astype(jnp.bfloat16).astype(jnp.float32)
            st = jnp.concatenate([mr, hi, tr - hi, jnp.zeros((5, D), jnp.float32)], axis=0)
            out_ref[j * (G // hp) + d0, 64:72, :] = st.astype(jnp.bfloat16)
    nt = T // tile
    K = lambda *a: [('k', i) for i in a]
    V = lambda *a: [('v', i) for i in a]
    waits = {0: K(0), 1: K(1) + V(0), 2: K(2, 3) + V(1, 2), 4: K(4, 5) + V(3, 4), 6: K(6, 7) + V(5, 6, 7)}
    plan = {0: K(2, 3) + V(1, 2), 1: K(4, 5) + V(3, 4), 3: K(6, 7) + V(5, 6, 7)}
    for j in range(H + 1):
        for c in range(nt):
            if j < H:
                if c == 0:
                    if j == 1:
                        load_own.wait()
                    for which, i in waits.get(j, ()):
                        (load_k if which == 'k' else load_v)[i].wait()
                    for which, i in plan.get(j, ()):
                        (load_k if which == 'k' else load_v)[i].start()
                scores(j, c)
            if j == H and c == 0:
                for which, i in waits.get(j, ()):
                    (load_k if which == 'k' else load_v)[i].wait()
            if j > 0:
                weigh(j - 1, c)
        if j > 0:
            finish(j - 1)

def attn(n, qg, k, v, own, tile=256, nbuf=2):
    S, HQ, D = qg.shape
    H, T, _ = k.shape
    nd = HQ * S // 64
    vm = pl.BlockSpec(memory_space=pltpu.VMEM)
    hbm = pl.BlockSpec(memory_space=pltpu.HBM)
    return pl.pallas_call(
        functools.partial(attn_kernel, cs=LOG2E / math.sqrt(D), tile=tile, nbuf=nbuf),
        in_specs=[pl.BlockSpec(memory_space=pltpu.SMEM)] + [hbm] * 4,
        out_specs=vm,
        out_shape=jax.ShapeDtypeStruct((nd, 72, D), jnp.bfloat16),
        scratch_shapes=[pltpu.VMEM(qg.shape, qg.dtype), pltpu.VMEM(own.shape, own.dtype), pltpu.SemaphoreType.DMA, pltpu.SemaphoreType.DMA, pltpu.VMEM((S * HQ, D), jnp.float32), pltpu.VMEM((H, T, D), jnp.bfloat16), pltpu.VMEM((H, T, D), jnp.bfloat16), pltpu.VMEM((T, D), jnp.bfloat16),
                        pltpu.SemaphoreType.DMA((H,)), pltpu.SemaphoreType.DMA((H,))] + [pltpu.VMEM((S * HQ // H, T), jnp.float32)] * nbuf,
        compiler_params=pltpu.CompilerParams(vmem_limit_bytes=63_300_000),
        cost_estimate=pl.CostEstimate(flops=2 << 30, bytes_accessed=12 << 20, transcendentals=4 << 20),
        name="attn",
    )(n, qg, k, v, own)

def combine_kernel(r_ref, o_ref, st_s):
    B = r_ref.shape[0]
    D = r_ref.shape[2]
    st_s[...] = r_ref[:, 64:72, :].astype(jnp.float32).reshape(B * 8, D)
    m = st_s[pl.ds(0, B, stride=8), :]
    t = st_s[pl.ds(1, B, stride=8), :] + st_s[pl.ds(2, B, stride=8), :]
    M = jnp.max(m, axis=0, keepdims=True)
    f = jnp.exp2(m - M)
    den = jnp.sum(f * t, axis=0, keepdims=True)
    lane = lax.broadcasted_iota(jnp.int32, (B, D), 1)
    f = jnp.where(lane < 64, f / den, 0.0)
    ft = jnp.transpose(jnp.concatenate([f, jnp.zeros((D - B, D), jnp.float32)], axis=0))[:64]
    acc = jnp.zeros((64, D), jnp.float32)
    for b in range(B):
        acc = acc + r_ref[b, 0:64, :].astype(jnp.float32) * ft[:, b:b + 1]
    res = jnp.concatenate([acc[:32], acc[32:]], axis=1).astype(jnp.bfloat16)
    for g in range(o_ref.shape[0]):
        o_ref[g] = res

def combine(r, copies):
    B, _, D = r.shape
    return pl.pallas_call(
        combine_kernel,
        in_specs=[pl.BlockSpec(memory_space=pltpu.VMEM)],
        out_specs=pl.BlockSpec(memory_space=pltpu.VMEM),
        out_shape=jax.ShapeDtypeStruct((copies, 32, 2 * D), jnp.bfloat16),
        scratch_shapes=[pltpu.VMEM((B * 8, D), jnp.float32)],
        compiler_params=pltpu.CompilerParams(vmem_limit_bytes=10 << 20),
        cost_estimate=pl.CostEstimate(flops=1 << 20, bytes_accessed=1 << 20, transcendentals=0),
        name="combine",
    )(r)

def spread_kernel(q_ref, o_ref):
    M, HQ, D = o_ref.shape
    q = q_ref[...].astype(jnp.float32)
    x = jnp.concatenate([q[:, h * D:(h + 1) * D] for h in range(HQ)], axis=0).astype(jnp.bfloat16)
    for i in range(M):
        o_ref[i] = x

def spread(q, members, width):
    vm = pl.BlockSpec(memory_space=pltpu.VMEM)
    return pl.pallas_call(
        spread_kernel, in_specs=[vm], out_specs=vm,
        out_shape=jax.ShapeDtypeStruct((members, q.shape[1] // width, width), q.dtype),
        compiler_params=pltpu.CompilerParams(vmem_limit_bytes=10 << 20),
        cost_estimate=pl.CostEstimate(flops=1 << 18, bytes_accessed=1 << 19, transcendentals=0),
        name="spread",
    )(q)

def body(query, prompt_code_cache, prompt_scale_cache, prefix_len, sample_key_value_cache, suffix_len, w_out):
    head_width = prompt_code_cache.shape[3]
    members = lax.axis_size("prefix")
    groups = lax.axis_size("samples")

    def swap(x, axis):
        return lax.all_to_all(x, axis, split_axis=0, concat_axis=0, tiled=True)

    gathered = swap(spread(query, members, head_width), "prefix")
    keys, values, own = prep(prefix_len, suffix_len, prompt_scale_cache, prompt_code_cache, query, sample_key_value_cache)
    partials = attn(prefix_len, gathered, keys, values, own)
    attention = combine(swap(partials, "prefix"), groups)
    rows = swap(attention, "samples").reshape(-1, attention.shape[2])
    terms = jnp.dot(rows, w_out, preferred_element_type=jnp.float32).astype(jnp.bfloat16)
    terms = swap(terms.reshape(members, -1, terms.shape[1]), "prefix")
    return jnp.sum(terms.astype(jnp.float32), axis=0).astype(jnp.bfloat16)


def solution(mesh):
    in_specs = (
        P(("samples", "prefix"), None),
        P(None, "prefix", None, None),
        P(None, "prefix", None),
        P(),
        P(("samples", "prefix"), None, None, None),
        P(("samples", "prefix")),
        P("prefix", "samples"),
    )
    return jax.shard_map(body, mesh=mesh, in_specs=in_specs, out_specs=P("prefix", "samples"), check_vma=False)
```

```python
import math, functools
import jax, jax.numpy as jnp
from jax import lax
from jax.experimental import pallas as pl
from jax.experimental.pallas import tpu as pltpu
from jax.sharding import PartitionSpec as P
LOG2E = 1.4426950408889634
FLOOR = -(2.0 ** 127)

def valid_rows(plen_ref, chunk):
    return jnp.clip(plen_ref[0] - lax.axis_index("prefix") * chunk, 0, chunk)

def prep_kernel(plen_ref, len_ref, scale_ref, code_hbm, q_ref, cache_hbm, kv_hbm, own_hbm, own_ref, own_sem, code_s, cache_s, k_s, v_s, hot_s, sc_v, sc_ref, sc_sem, in_sem, cache_sem, k_sem, v_sem, *, tb, sb, cs):
    H, T, lanes = k_s.shape
    G = own_ref.shape[1] // H
    steps = k_s.shape[1] // tb

    def rows(i, size):
        return pl.ds(pl.multiple_of(i * size, size), size)

    def load(i):
        return pltpu.make_async_copy(code_hbm.at[:, rows(i, tb * H), :], code_s.at[:, rows(i, tb * H), :], in_sem.at[i])

    def save(i):
        at = rows(i, tb)
        return (pltpu.make_async_copy(k_s.at[:, at, :], kv_hbm.at[0, :, at, :], k_sem.at[i]),
                pltpu.make_async_copy(v_s.at[:, at, :], kv_hbm.at[1, :, at, :], v_sem.at[i]))

    cache_copy = pltpu.make_async_copy(cache_hbm, cache_s, cache_sem)
    load(0).start()
    cache_copy.start()
    for i in range(1, steps):
        load(i).start()
    B = scale_ref.shape[2]
    for c in range(2):
        sc_v[c * H:(c + 1) * H, 0:B] = scale_ref[c].astype(jnp.float32)
    sc_copy = pltpu.make_async_copy(sc_v, sc_ref, sc_sem)
    sc_copy.start()
    n = valid_rows(plen_ref, T)
    hr = hot_s.shape[0]
    half = sb // 2
    r = lax.broadcasted_iota(jnp.int32, (hr, hr), 0)
    c = lax.broadcasted_iota(jnp.int32, (hr, hr), 1)
    hot_s[...] = jnp.where((r % half) * H + r // half == c, 1.0, 0.0).astype(jnp.bfloat16)

    sc_copy.wait()

    @pl.loop(0, steps)
    def _(i):
        load(i).wait()
        prep_step(i, n, sc_ref, code_s, k_s, v_s, hot_s, tb=tb, sb=sb)
        for copy in save(i):
            copy.start()

    cache_copy.wait()
    q = q_ref[...].astype(jnp.float32)
    for i in range(H):
        own = jnp.concatenate([q[:, h * lanes:(h + 1) * lanes] for h in range(i * G, (i + 1) * G)], axis=0).astype(jnp.bfloat16)
        cols = slice(i * lanes, (i + 1) * lanes)
        grp = slice(i * G, (i + 1) * G)
        C = cache_s.shape[2]
        s = lax.dot_general(own, cache_s[0, 0, :, cols], (((1,), (1,)), ((), ())), preferred_element_type=jnp.float32) * cs
        s = jnp.where(lax.broadcasted_iota(jnp.int32, (G, C), 1) < len_ref[0], s, -jnp.inf)
        m = jnp.max(s, axis=1, keepdims=True)
        w = jnp.exp2(s - m).astype(jnp.bfloat16)
        own_ref[0, grp, :] = jnp.dot(w, cache_s[0, 1, :, cols], preferred_element_type=jnp.float32)
        own_ref[1, grp, :] = jnp.broadcast_to(m, (G, lanes))
        own_ref[2, grp, :] = jnp.broadcast_to(jnp.sum(w.astype(jnp.float32), axis=1, keepdims=True), (G, lanes))
    own_copy = pltpu.make_async_copy(own_ref, own_hbm.at[0:3], own_sem)
    own_copy.start()
    for i in range(steps):
        for copy in save(i):
            copy.wait()
    own_copy.wait()


def prep_step(i, n, sc_ref, code_ref, k_ref, v_ref, hot_s, *, tb, sb):
    heads = k_ref.shape[0]
    lanes = code_ref.shape[2]
    half = sb // 2
    hr = half * heads

    def move(c, b):
        x = jnp.concatenate([code_ref[c, pl.ds(pl.multiple_of(i * tb * heads, tb * heads) + (2 * b + u) * hr, hr), :] for u in range(2)], axis=1)
        y = jnp.dot(hot_s[...], x, preferred_element_type=jnp.float32)
        blk = i * (tb // sb) + b
        return [y[j * half:(j + 1) * half] * sc_ref[c * heads + j, blk] for j in range(heads)]

    def go(masked):
        for b in range(tb // sb):
            rows = [pl.ds(pl.multiple_of(i * tb, tb) + b * sb + u * half, half) for u in range(2)]
            if masked:
                left = n - i * tb - b * sb
                ok = [lax.broadcasted_iota(jnp.int32, (half, lanes), 0) + u * half < left for u in range(2)]
            for c in range(2):
                ys = move(c, b)
                if masked and c == 0 and b == 0:
                    first = [y[0:1, 0:lanes] for y in ys]
                for j in range(heads):
                    for u in range(2):
                        y = ys[j][:, u * lanes:(u + 1) * lanes]
                        if c == 0:
                            if masked:
                                y = jnp.where(ok[u], y, first[j])
                            k_ref[j, rows[u], :] = y.astype(jnp.bfloat16)
                        else:
                            if masked:
                                y = jnp.where(ok[u], y, 0.0)
                            v_ref[j, rows[u], :] = y.astype(jnp.bfloat16)

    whole = (i + 1) * tb <= n
    some = i * tb < n

    @pl.when(whole)
    def _():
        go(False)

    @pl.when(jnp.logical_and(some, jnp.logical_not(whole)))
    def _():
        go(True)

    @pl.when(jnp.logical_not(some))
    def _():
        for j in range(heads):
            k_ref[j, pl.ds(pl.multiple_of(i * tb, tb), tb), :] = jnp.broadcast_to(jnp.where(i == 0, 0.0, k_ref[j, 0:16].astype(jnp.float32)[0:1]), (tb, lanes)).astype(jnp.bfloat16)
            v_ref[j, pl.ds(pl.multiple_of(i * tb, tb), tb), :] = jnp.zeros((tb, lanes), jnp.bfloat16)

def prep(n, length, scale, code, q, cache):
    _, T, H, D = code.shape
    tb = T // 8
    sb = T // scale.shape[1]
    G = q.shape[1] // (H * D)
    smem = pl.BlockSpec(memory_space=pltpu.SMEM)
    vmem = pl.BlockSpec(memory_space=pltpu.VMEM)
    hbm = pl.BlockSpec(memory_space=pltpu.HBM)
    return pl.pallas_call(
        functools.partial(prep_kernel, tb=tb, sb=sb, cs=LOG2E / math.sqrt(D)),
        in_specs=[smem, smem, vmem, hbm, vmem, hbm],
        out_specs=[hbm, hbm],
        out_shape=[jax.ShapeDtypeStruct((4, H, T, D), jnp.bfloat16)] + [jax.ShapeDtypeStruct((480, H * G, D), jnp.float32)],
        scratch_shapes=[pltpu.VMEM((3, H * G, D), jnp.float32), pltpu.SemaphoreType.DMA, pltpu.VMEM((2, T * H, D), jnp.bfloat16), pltpu.VMEM(cache.shape, jnp.bfloat16),
                        pltpu.VMEM((H, T, D), jnp.bfloat16), pltpu.VMEM((H, T, D), jnp.bfloat16),
                        pltpu.VMEM((sb // 2 * H, sb // 2 * H), jnp.bfloat16),
                        pltpu.VMEM((2 * H, 128), jnp.float32), pltpu.SMEM((2 * H, 128), jnp.float32), pltpu.SemaphoreType.DMA,
                        pltpu.SemaphoreType.DMA((T // tb,)), pltpu.SemaphoreType.DMA,
                        pltpu.SemaphoreType.DMA((T // tb,)), pltpu.SemaphoreType.DMA((T // tb,))],
        compiler_params=pltpu.CompilerParams(vmem_limit_bytes=63_300_000),
        cost_estimate=pl.CostEstimate(flops=16 << 20, bytes_accessed=20 << 20, transcendentals=0),
        name="prep",
    )(n, length, scale.transpose(0, 2, 1), code.reshape(2, T * H, D), q, cache)

def attn_kernel(plen_ref, qg_ref, kv_hbm, own_hbm, out_ref, own_ref, own_sem, q_s, k_ref, v_ref, one_s, k_sem, v_sem, *s_s, cs, tile, nbuf):
    S, HQ, D = qg_ref.shape
    _, H, T, _ = kv_hbm.shape
    G = HQ // H
    n = valid_rows(plen_ref, T)
    me = lax.axis_index("prefix")
    R = G * S
    hp = 64 // S
    load_k = [pltpu.make_async_copy(kv_hbm.at[0, j], k_ref.at[j], k_sem.at[j]) for j in range(H)]
    load_v = [pltpu.make_async_copy(kv_hbm.at[1, j], v_ref.at[j], v_sem.at[j]) for j in range(H)]
    load_own = pltpu.make_async_copy(own_hbm.at[0:3], own_ref, own_sem)
    load_k[0].start()
    load_k[1].start()
    load_v[0].start()
    load_own.start()
    one_s[...] = jnp.where(lax.broadcasted_iota(jnp.int32, (T, D), 0) < n, 1.0, 0.0).astype(jnp.bfloat16)
    sidx = lax.broadcasted_iota(jnp.int32, (S, D), 0)
    q_s[...] = qg_ref[...].astype(jnp.float32).reshape(S * HQ, D)
    ms = {}
    def scores(j, c):
        if c == 0:
            q = jnp.concatenate([q_s[pl.ds(j * G + h, S, stride=HQ), :] for h in range(G)], axis=0).astype(jnp.bfloat16)
            ms[j] = [q, None]
        q = ms[j][0]
        z = lax.dot_general(q, k_ref[j, c * tile:(c + 1) * tile, :], (((1,), (1,)), ((), ())), preferred_element_type=jnp.float32)
        s_s[j % nbuf][:, c * tile:(c + 1) * tile] = z
        m = ms[j][1]
        for l in range(tile // D):
            zz = z[:, l * D:(l + 1) * D]
            m = zz if m is None else jnp.maximum(m, zz)
        ms[j][1] = m
        if (c + 1) * tile == T:
            m = jnp.max(m, axis=1, keepdims=True) * cs
            ms[j][1] = jnp.broadcast_to(m, (R, D)).astype(jnp.bfloat16).astype(jnp.float32)
    acc = {}
    def weigh(j, c):
        m = ms[j][1]
        z = s_s[j % nbuf][:, c * tile:(c + 1) * tile]
        p = jnp.exp2(z * cs - jnp.concatenate([m] * (tile // D), axis=1)).astype(jnp.bfloat16)
        at = slice(c * tile, (c + 1) * tile)
        o = jnp.dot(p, jnp.concatenate([v_ref[j, at, :], one_s[at, :]], axis=1), preferred_element_type=jnp.float32)
        acc[j] = o if c == 0 else acc[j] + o
    def finish(j):
        o = acc[j][:, :D]
        tot = acc[j][:, D:]
        m = jnp.where(n > 0, ms[j][1], FLOOR)
        mts = []
        for h in range(G):
            sl = slice(h * S, (h + 1) * S)
            r = j * G + h
            mine = sidx == me
            sm2 = jnp.where(mine, own_ref[1, r:r + 1, :], FLOOR)
            mn = jnp.maximum(m[sl], sm2).astype(jnp.bfloat16).astype(jnp.float32)
            fa = jnp.exp2(m[sl] - mn)
            fb = jnp.where(mine, jnp.exp2(sm2 - mn), 0.0)
            on = o[sl] * fa + own_ref[0, r:r + 1, :] * fb
            tn = tot[sl] * fa + own_ref[2, r:r + 1, :] * fb
            d, hd = divmod(r, hp)
            out_ref[d, hd * S:(hd + 1) * S, :] = on.astype(jnp.bfloat16)
            mts.append((mn, tn))
        diag = lax.broadcasted_iota(jnp.int32, (64, D), 0) == lax.broadcasted_iota(jnp.int32, (64, D), 1)
        for d0 in range(G // hp):
            mm = jnp.concatenate([a for a, _ in mts[d0 * hp:(d0 + 1) * hp]], axis=0)
            tt = jnp.concatenate([b for _, b in mts[d0 * hp:(d0 + 1) * hp]], axis=0)
            mr = jnp.sum(jnp.where(diag, mm, 0.0), axis=0, keepdims=True)
            tr = jnp.sum(jnp.where(diag, tt, 0.0), axis=0, keepdims=True)
            hi = tr.astype(jnp.bfloat16).astype(jnp.float32)
            st = jnp.concatenate([mr, hi, tr - hi, jnp.zeros((5, D), jnp.float32)], axis=0)
            out_ref[j * (G // hp) + d0, 64:72, :] = st.astype(jnp.bfloat16)
    nt = T // tile
    K = lambda *a: [('k', i) for i in a]
    V = lambda *a: [('v', i) for i in a]
    waits = {0: K(0), 1: K(1) + V(0), 2: K(2, 3) + V(1, 2), 4: K(4, 5) + V(3, 4), 6: K(6, 7) + V(5, 6, 7)}
    plan = {0: K(2, 3) + V(1, 2), 1: K(4, 5) + V(3, 4), 3: K(6, 7) + V(5, 6, 7)}
    for j in range(H + 1):
        for c in range(nt):
            if j < H:
                if c == 0:
                    if j == 1:
                        load_own.wait()
                    for which, i in waits.get(j, ()):
                        (load_k if which == 'k' else load_v)[i].wait()
                    for which, i in plan.get(j, ()):
                        (load_k if which == 'k' else load_v)[i].start()
                scores(j, c)
            if j == H and c == 0:
                for which, i in waits.get(j, ()):
                    (load_k if which == 'k' else load_v)[i].wait()
            if j > 0:
                weigh(j - 1, c)
        if j > 0:
            finish(j - 1)

def attn(n, qg, kv, own, tile=256, nbuf=2):
    S, HQ, D = qg.shape
    _, H, T, _ = kv.shape
    nd = HQ * S // 64
    vm = pl.BlockSpec(memory_space=pltpu.VMEM)
    hbm = pl.BlockSpec(memory_space=pltpu.HBM)
    return pl.pallas_call(
        functools.partial(attn_kernel, cs=LOG2E / math.sqrt(D), tile=tile, nbuf=nbuf),
        in_specs=[pl.BlockSpec(memory_space=pltpu.SMEM), vm, hbm, hbm],
        out_specs=vm,
        out_shape=jax.ShapeDtypeStruct((nd, 72, D), jnp.bfloat16),
        scratch_shapes=[pltpu.VMEM((3,) + own.shape[1:], own.dtype), pltpu.SemaphoreType.DMA, pltpu.VMEM((S * HQ, D), jnp.float32), pltpu.VMEM((H, T, D), jnp.bfloat16), pltpu.VMEM((H, T, D), jnp.bfloat16), pltpu.VMEM((T, D), jnp.bfloat16),
                        pltpu.SemaphoreType.DMA((H,)), pltpu.SemaphoreType.DMA((H,))] + [pltpu.VMEM((S * HQ // H, T), jnp.float32)] * nbuf,
        compiler_params=pltpu.CompilerParams(vmem_limit_bytes=48_000_000),
        cost_estimate=pl.CostEstimate(flops=2 << 30, bytes_accessed=12 << 20, transcendentals=4 << 20),
        name="attn",
    )(n, qg, kv, own)

def combine_kernel(r_ref, o_ref, st_s):
    B = r_ref.shape[0]
    D = r_ref.shape[2]
    st_s[...] = r_ref[:, 64:72, :].astype(jnp.float32).reshape(B * 8, D)
    m = st_s[pl.ds(0, B, stride=8), :]
    t = st_s[pl.ds(1, B, stride=8), :] + st_s[pl.ds(2, B, stride=8), :]
    M = jnp.max(m, axis=0, keepdims=True)
    f = jnp.exp2(m - M)
    den = jnp.sum(f * t, axis=0, keepdims=True)
    lane = lax.broadcasted_iota(jnp.int32, (B, D), 1)
    f = jnp.where(lane < 64, f / den, 0.0)
    ft = jnp.transpose(jnp.concatenate([f, jnp.zeros((D - B, D), jnp.float32)], axis=0))[:64]
    acc = jnp.zeros((64, D), jnp.float32)
    for b in range(B):
        acc = acc + r_ref[b, 0:64, :].astype(jnp.float32) * ft[:, b:b + 1]
    res = jnp.concatenate([acc[:32], acc[32:]], axis=1).astype(jnp.bfloat16)
    for g in range(o_ref.shape[0]):
        o_ref[g] = res

def combine(r, copies):
    B, _, D = r.shape
    return pl.pallas_call(
        combine_kernel,
        in_specs=[pl.BlockSpec(memory_space=pltpu.VMEM)],
        out_specs=pl.BlockSpec(memory_space=pltpu.VMEM),
        out_shape=jax.ShapeDtypeStruct((copies, 32, 2 * D), jnp.bfloat16),
        scratch_shapes=[pltpu.VMEM((B * 8, D), jnp.float32)],
        compiler_params=pltpu.CompilerParams(vmem_limit_bytes=10 << 20),
        cost_estimate=pl.CostEstimate(flops=1 << 20, bytes_accessed=1 << 20, transcendentals=0),
        name="combine",
    )(r)

def spread_kernel(q_ref, o_ref):
    M, HQ, D = o_ref.shape
    q = q_ref[...].astype(jnp.float32)
    x = jnp.concatenate([q[:, h * D:(h + 1) * D] for h in range(HQ)], axis=0).astype(jnp.bfloat16)
    for i in range(M):
        o_ref[i] = x

def spread(q, members, width):
    vm = pl.BlockSpec(memory_space=pltpu.VMEM)
    return pl.pallas_call(
        spread_kernel, in_specs=[vm], out_specs=vm,
        out_shape=jax.ShapeDtypeStruct((members, q.shape[1] // width, width), q.dtype),
        compiler_params=pltpu.CompilerParams(vmem_limit_bytes=10 << 20),
        cost_estimate=pl.CostEstimate(flops=1 << 18, bytes_accessed=1 << 19, transcendentals=0),
        name="spread",
    )(q)

def body(query, prompt_code_cache, prompt_scale_cache, prefix_len, sample_key_value_cache, suffix_len, w_out):
    head_width = prompt_code_cache.shape[3]
    members = lax.axis_size("prefix")
    groups = lax.axis_size("samples")

    def swap(x, axis):
        return lax.all_to_all(x, axis, split_axis=0, concat_axis=0, tiled=True)

    gathered = swap(spread(query, members, head_width), "prefix")
    keys_values, own = prep(prefix_len, suffix_len, prompt_scale_cache, prompt_code_cache, query, sample_key_value_cache)
    partials = attn(prefix_len, gathered, keys_values, own)
    attention = combine(swap(partials, "prefix"), groups)
    rows = swap(attention, "samples").reshape(-1, attention.shape[2])
    terms = jnp.dot(rows, w_out, preferred_element_type=jnp.float32).astype(jnp.bfloat16)
    terms = swap(terms.reshape(members, -1, terms.shape[1]), "prefix")
    return jnp.sum(terms.astype(jnp.float32), axis=0).astype(jnp.bfloat16)


def solution(mesh):
    in_specs = (
        P(("samples", "prefix"), None),
        P(None, "prefix", None, None),
        P(None, "prefix", None),
        P(),
        P(("samples", "prefix"), None, None, None),
        P(("samples", "prefix")),
        P("prefix", "samples"),
    )
    return jax.shard_map(body, mesh=mesh, in_specs=in_specs, out_specs=P("prefix", "samples"), check_vma=False)
```

```python
import math, functools
import jax, jax.numpy as jnp
from jax import lax
from jax.experimental import pallas as pl
from jax.experimental.pallas import tpu as pltpu
from jax.sharding import PartitionSpec as P
LOG2E = 1.4426950408889634
FLOOR = -(2.0 ** 127)

def valid_rows(plen_ref, chunk):
    return jnp.clip(plen_ref[0] - lax.axis_index("prefix") * chunk, 0, chunk)

def prep_kernel(plen_ref, len_ref, scale_ref, code_hbm, q_ref, cache_hbm, kv_hbm, own_hbm, own_ref, own_sem, code_s, cache_s, k_s, v_s, hot_s, sc_v, sc_ref, sc_sem, in_sem, cache_sem, k_sem, v_sem, *, tb, sb, cs):
    H, T, lanes = k_s.shape
    G = own_ref.shape[1] // H
    steps = k_s.shape[1] // tb

    def rows(i, size):
        return pl.ds(pl.multiple_of(i * size, size), size)

    def load(i):
        return pltpu.make_async_copy(code_hbm.at[:, rows(i, tb * H), :], code_s.at[:, rows(i, tb * H), :], in_sem.at[i])

    def save(i):
        at = rows(i, tb)
        return (pltpu.make_async_copy(k_s.at[:, at, :], kv_hbm.at[0, :, at, :], k_sem.at[i]),
                pltpu.make_async_copy(v_s.at[:, at, :], kv_hbm.at[1, :, at, :], v_sem.at[i]))

    cache_copy = pltpu.make_async_copy(cache_hbm, cache_s, cache_sem)
    load(0).start()
    cache_copy.start()
    for i in range(1, steps):
        load(i).start()
    B = scale_ref.shape[2]
    for c in range(2):
        sc_v[c * H:(c + 1) * H, 0:B] = scale_ref[c].astype(jnp.float32)
    sc_copy = pltpu.make_async_copy(sc_v, sc_ref, sc_sem)
    sc_copy.start()
    n = valid_rows(plen_ref, T)
    hr = hot_s.shape[0]
    half = sb // 2
    r = lax.broadcasted_iota(jnp.int32, (hr, hr), 0)
    c = lax.broadcasted_iota(jnp.int32, (hr, hr), 1)
    hot_s[...] = jnp.where((r % half) * H + r // half == c, 1.0, 0.0).astype(jnp.bfloat16)

    sc_copy.wait()

    @pl.loop(0, steps)
    def _(i):
        load(i).wait()
        prep_step(i, n, sc_ref, code_s, k_s, v_s, hot_s, tb=tb, sb=sb)
        for copy in save(i):
            copy.start()

    cache_copy.wait()
    q = q_ref[...].astype(jnp.float32)
    for i in range(H):
        own = jnp.concatenate([q[:, h * lanes:(h + 1) * lanes] for h in range(i * G, (i + 1) * G)], axis=0).astype(jnp.bfloat16)
        cols = slice(i * lanes, (i + 1) * lanes)
        grp = slice(i * G, (i + 1) * G)
        C = cache_s.shape[2]
        s = lax.dot_general(own, cache_s[0, 0, :, cols], (((1,), (1,)), ((), ())), preferred_element_type=jnp.float32) * cs
        s = jnp.where(lax.broadcasted_iota(jnp.int32, (G, C), 1) < len_ref[0], s, -jnp.inf)
        m = jnp.max(s, axis=1, keepdims=True)
        w = jnp.exp2(s - m).astype(jnp.bfloat16)
        own_ref[0, grp, :] = jnp.dot(w, cache_s[0, 1, :, cols], preferred_element_type=jnp.float32)
        own_ref[1, grp, :] = jnp.broadcast_to(m, (G, lanes))
        own_ref[2, grp, :] = jnp.broadcast_to(jnp.sum(w.astype(jnp.float32), axis=1, keepdims=True), (G, lanes))
    own_copy = pltpu.make_async_copy(own_ref, own_hbm.at[0:3], own_sem)
    own_copy.start()
    for i in range(steps):
        for copy in save(i):
            copy.wait()
    own_copy.wait()


def prep_step(i, n, sc_ref, code_ref, k_ref, v_ref, hot_s, *, tb, sb):
    heads = k_ref.shape[0]
    lanes = code_ref.shape[2]
    half = sb // 2
    hr = half * heads

    def move(c, b):
        x = jnp.concatenate([code_ref[c, pl.ds(pl.multiple_of(i * tb * heads, tb * heads) + (2 * b + u) * hr, hr), :] for u in range(2)], axis=1)
        y = jnp.dot(hot_s[...], x, preferred_element_type=jnp.float32)
        blk = i * (tb // sb) + b
        return [y[j * half:(j + 1) * half] * sc_ref[c * heads + j, blk] for j in range(heads)]

    def go(masked):
        for b in range(tb // sb):
            rows = [pl.ds(pl.multiple_of(i * tb, tb) + b * sb + u * half, half) for u in range(2)]
            if masked:
                left = n - i * tb - b * sb
                ok = [lax.broadcasted_iota(jnp.int32, (half, lanes), 0) + u * half < left for u in range(2)]
            for c in range(2):
                ys = move(c, b)
                if masked and c == 0 and b == 0:
                    first = [y[0:1, 0:lanes] for y in ys]
                for j in range(heads):
                    for u in range(2):
                        y = ys[j][:, u * lanes:(u + 1) * lanes]
                        if c == 0:
                            if masked:
                                y = jnp.where(ok[u], y, first[j])
                            k_ref[j, rows[u], :] = y.astype(jnp.bfloat16)
                        else:
                            if masked:
                                y = jnp.where(ok[u], y, 0.0)
                            v_ref[j, rows[u], :] = y.astype(jnp.bfloat16)

    whole = (i + 1) * tb <= n
    some = i * tb < n

    @pl.when(whole)
    def _():
        go(False)

    @pl.when(jnp.logical_and(some, jnp.logical_not(whole)))
    def _():
        go(True)

    @pl.when(jnp.logical_not(some))
    def _():
        for j in range(heads):
            k_ref[j, pl.ds(pl.multiple_of(i * tb, tb), tb), :] = jnp.broadcast_to(jnp.where(i == 0, 0.0, k_ref[j, 0:16].astype(jnp.float32)[0:1]), (tb, lanes)).astype(jnp.bfloat16)
            v_ref[j, pl.ds(pl.multiple_of(i * tb, tb), tb), :] = jnp.zeros((tb, lanes), jnp.bfloat16)

def prep(n, length, scale, code, q, cache):
    _, T, H, D = code.shape
    tb = T // 8
    sb = T // scale.shape[1]
    G = q.shape[1] // (H * D)
    smem = pl.BlockSpec(memory_space=pltpu.SMEM)
    vmem = pl.BlockSpec(memory_space=pltpu.VMEM)
    hbm = pl.BlockSpec(memory_space=pltpu.HBM)
    return pl.pallas_call(
        functools.partial(prep_kernel, tb=tb, sb=sb, cs=LOG2E / math.sqrt(D)),
        in_specs=[smem, smem, vmem, hbm, vmem, hbm],
        out_specs=[hbm, hbm],
        out_shape=[jax.ShapeDtypeStruct((4, H, T, D), jnp.bfloat16)] + [jax.ShapeDtypeStruct((480, H * G, D), jnp.float32)],
        scratch_shapes=[pltpu.VMEM((3, H * G, D), jnp.float32), pltpu.SemaphoreType.DMA, pltpu.VMEM((2, T * H, D), jnp.bfloat16), pltpu.VMEM(cache.shape, jnp.bfloat16),
                        pltpu.VMEM((H, T, D), jnp.bfloat16), pltpu.VMEM((H, T, D), jnp.bfloat16),
                        pltpu.VMEM((sb // 2 * H, sb // 2 * H), jnp.bfloat16),
                        pltpu.VMEM((2 * H, 128), jnp.float32), pltpu.SMEM((2 * H, 128), jnp.float32), pltpu.SemaphoreType.DMA,
                        pltpu.SemaphoreType.DMA((T // tb,)), pltpu.SemaphoreType.DMA,
                        pltpu.SemaphoreType.DMA((T // tb,)), pltpu.SemaphoreType.DMA((T // tb,))],
        compiler_params=pltpu.CompilerParams(vmem_limit_bytes=63_300_000),
        cost_estimate=pl.CostEstimate(flops=16 << 20, bytes_accessed=20 << 20, transcendentals=0),
        name="prep",
    )(n, length, scale.transpose(0, 2, 1), code.reshape(2, T * H, D), q, cache)

def attn_kernel(plen_ref, qg_ref, kv_hbm, own_hbm, out_ref, own_ref, own_sem, q_s, k_ref, v_ref, one_s, k_sem, v_sem, *s_s, cs, tile, nbuf):
    S, HQ, D = qg_ref.shape
    _, H, T, _ = kv_hbm.shape
    G = HQ // H
    n = valid_rows(plen_ref, T)
    me = lax.axis_index("prefix")
    R = G * S
    hp = 64 // S
    load_k = [pltpu.make_async_copy(kv_hbm.at[0, j], k_ref.at[j], k_sem.at[j]) for j in range(H)]
    load_v = [pltpu.make_async_copy(kv_hbm.at[1, j], v_ref.at[j], v_sem.at[j]) for j in range(H)]
    load_own = pltpu.make_async_copy(own_hbm.at[0:3], own_ref, own_sem)
    load_k[0].start()
    load_k[1].start()
    load_v[0].start()
    load_own.start()
    one_s[...] = jnp.where(lax.broadcasted_iota(jnp.int32, (T, D), 0) < n, 1.0, 0.0).astype(jnp.bfloat16)
    sidx = lax.broadcasted_iota(jnp.int32, (S, D), 0)
    q_s[...] = qg_ref[...].astype(jnp.float32).reshape(S * HQ, D)
    ms = {}
    def scores(j, c):
        if c == 0:
            q = jnp.concatenate([q_s[pl.ds(j * G + h, S, stride=HQ), :] for h in range(G)], axis=0).astype(jnp.bfloat16)
            ms[j] = [q, None]
        q = ms[j][0]
        z = lax.dot_general(q, k_ref[j, c * tile:(c + 1) * tile, :], (((1,), (1,)), ((), ())), preferred_element_type=jnp.float32)
        s_s[j % nbuf][:, c * tile:(c + 1) * tile] = z
        m = ms[j][1]
        for l in range(tile // D):
            zz = z[:, l * D:(l + 1) * D]
            m = zz if m is None else jnp.maximum(m, zz)
        ms[j][1] = m
        if (c + 1) * tile == T:
            m = jnp.max(m, axis=1, keepdims=True) * cs
            ms[j][1] = jnp.broadcast_to(m, (R, D)).astype(jnp.bfloat16).astype(jnp.float32)
    acc = {}
    part = {}
    def weigh(j, c):
        half = R // 2
        wide = 2 * tile
        h, cc = c % 2, c // 2
        m = ms[j][1][h * half:(h + 1) * half]
        at = slice(cc * wide, (cc + 1) * wide)
        z = s_s[j % nbuf][h * half:(h + 1) * half, at]
        p = jnp.exp2(z * cs - jnp.concatenate([m] * (wide // D), axis=1)).astype(jnp.bfloat16)
        o = jnp.dot(p, jnp.concatenate([v_ref[j, at, :], one_s[at, :]], axis=1), preferred_element_type=jnp.float32)
        part[(j, h)] = o if cc == 0 else part[(j, h)] + o
        if (c + 1) * tile == T:
            acc[j] = jnp.concatenate([part[(j, 0)], part[(j, 1)]], axis=0)
    def finish(j):
        o = acc[j][:, :D]
        tot = acc[j][:, D:]
        m = jnp.where(n > 0, ms[j][1], FLOOR)
        mts = []
        for h in range(G):
            sl = slice(h * S, (h + 1) * S)
            r = j * G + h
            mine = sidx == me
            sm2 = jnp.where(mine, own_ref[1, r:r + 1, :], FLOOR)
            mn = jnp.maximum(m[sl], sm2).astype(jnp.bfloat16).astype(jnp.float32)
            fa = jnp.exp2(m[sl] - mn)
            fb = jnp.where(mine, jnp.exp2(sm2 - mn), 0.0)
            on = o[sl] * fa + own_ref[0, r:r + 1, :] * fb
            tn = tot[sl] * fa + own_ref[2, r:r + 1, :] * fb
            d, hd = divmod(r, hp)
            out_ref[d, hd * S:(hd + 1) * S, :] = on.astype(jnp.bfloat16)
            mts.append((mn, tn))
        diag = lax.broadcasted_iota(jnp.int32, (64, D), 0) == lax.broadcasted_iota(jnp.int32, (64, D), 1)
        for d0 in range(G // hp):
            mm = jnp.concatenate([a for a, _ in mts[d0 * hp:(d0 + 1) * hp]], axis=0)
            tt = jnp.concatenate([b for _, b in mts[d0 * hp:(d0 + 1) * hp]], axis=0)
            mr = jnp.sum(jnp.where(diag, mm, 0.0), axis=0, keepdims=True)
            tr = jnp.sum(jnp.where(diag, tt, 0.0), axis=0, keepdims=True)
            hi = tr.astype(jnp.bfloat16).astype(jnp.float32)
            st = jnp.concatenate([mr, hi, tr - hi, jnp.zeros((5, D), jnp.float32)], axis=0)
            out_ref[j * (G // hp) + d0, 64:72, :] = st.astype(jnp.bfloat16)
    nt = T // tile
    K = lambda *a: [('k', i) for i in a]
    V = lambda *a: [('v', i) for i in a]
    waits = {0: K(0), 1: K(1) + V(0), 2: K(2, 3) + V(1, 2), 4: K(4, 5) + V(3, 4), 6: K(6, 7) + V(5, 6, 7)}
    plan = {0: K(2, 3) + V(1, 2), 1: K(4, 5) + V(3, 4), 3: K(6, 7) + V(5, 6, 7)}
    for j in range(H + 1):
        for c in range(nt):
            if j < H:
                if c == 0:
                    if j == 1:
                        load_own.wait()
                    for which, i in waits.get(j, ()):
                        (load_k if which == 'k' else load_v)[i].wait()
                    for which, i in plan.get(j, ()):
                        (load_k if which == 'k' else load_v)[i].start()
                scores(j, c)
            if j == H and c == 0:
                for which, i in waits.get(j, ()):
                    (load_k if which == 'k' else load_v)[i].wait()
            if j > 0:
                weigh(j - 1, c)
        if j > 0:
            finish(j - 1)

def attn(n, qg, kv, own, tile=256, nbuf=2):
    S, HQ, D = qg.shape
    _, H, T, _ = kv.shape
    nd = HQ * S // 64
    vm = pl.BlockSpec(memory_space=pltpu.VMEM)
    hbm = pl.BlockSpec(memory_space=pltpu.HBM)
    return pl.pallas_call(
        functools.partial(attn_kernel, cs=LOG2E / math.sqrt(D), tile=tile, nbuf=nbuf),
        in_specs=[pl.BlockSpec(memory_space=pltpu.SMEM), vm, hbm, hbm],
        out_specs=vm,
        out_shape=jax.ShapeDtypeStruct((nd, 72, D), jnp.bfloat16),
        scratch_shapes=[pltpu.VMEM((3,) + own.shape[1:], own.dtype), pltpu.SemaphoreType.DMA, pltpu.VMEM((S * HQ, D), jnp.float32), pltpu.VMEM((H, T, D), jnp.bfloat16), pltpu.VMEM((H, T, D), jnp.bfloat16), pltpu.VMEM((T, D), jnp.bfloat16),
                        pltpu.SemaphoreType.DMA((H,)), pltpu.SemaphoreType.DMA((H,))] + [pltpu.VMEM((S * HQ // H, T), jnp.float32)] * nbuf,
        compiler_params=pltpu.CompilerParams(vmem_limit_bytes=48_000_000),
        cost_estimate=pl.CostEstimate(flops=2 << 30, bytes_accessed=12 << 20, transcendentals=4 << 20),
        name="attn",
    )(n, qg, kv, own)

def combine_kernel(r_ref, o_ref, st_s):
    B = r_ref.shape[0]
    D = r_ref.shape[2]
    st_s[...] = r_ref[:, 64:72, :].astype(jnp.float32).reshape(B * 8, D)
    m = st_s[pl.ds(0, B, stride=8), :]
    t = st_s[pl.ds(1, B, stride=8), :] + st_s[pl.ds(2, B, stride=8), :]
    M = jnp.max(m, axis=0, keepdims=True)
    f = jnp.exp2(m - M)
    den = jnp.sum(f * t, axis=0, keepdims=True)
    lane = lax.broadcasted_iota(jnp.int32, (B, D), 1)
    f = jnp.where(lane < 64, f / den, 0.0)
    ft = jnp.transpose(jnp.concatenate([f, jnp.zeros((D - B, D), jnp.float32)], axis=0))[:64]
    acc = jnp.zeros((64, D), jnp.float32)
    for b in range(B):
        acc = acc + r_ref[b, 0:64, :].astype(jnp.float32) * ft[:, b:b + 1]
    res = jnp.concatenate([acc[:32], acc[32:]], axis=1).astype(jnp.bfloat16)
    for g in range(o_ref.shape[0]):
        o_ref[g] = res

def combine(r, copies):
    B, _, D = r.shape
    return pl.pallas_call(
        combine_kernel,
        in_specs=[pl.BlockSpec(memory_space=pltpu.VMEM)],
        out_specs=pl.BlockSpec(memory_space=pltpu.VMEM),
        out_shape=jax.ShapeDtypeStruct((copies, 32, 2 * D), jnp.bfloat16),
        scratch_shapes=[pltpu.VMEM((B * 8, D), jnp.float32)],
        compiler_params=pltpu.CompilerParams(vmem_limit_bytes=10 << 20),
        cost_estimate=pl.CostEstimate(flops=1 << 20, bytes_accessed=1 << 20, transcendentals=0),
        name="combine",
    )(r)

def spread_kernel(q_ref, o_ref):
    M, HQ, D = o_ref.shape
    q = q_ref[...].astype(jnp.float32)
    x = jnp.concatenate([q[:, h * D:(h + 1) * D] for h in range(HQ)], axis=0).astype(jnp.bfloat16)
    for i in range(M):
        o_ref[i] = x

def spread(q, members, width):
    vm = pl.BlockSpec(memory_space=pltpu.VMEM)
    return pl.pallas_call(
        spread_kernel, in_specs=[vm], out_specs=vm,
        out_shape=jax.ShapeDtypeStruct((members, q.shape[1] // width, width), q.dtype),
        compiler_params=pltpu.CompilerParams(vmem_limit_bytes=10 << 20),
        cost_estimate=pl.CostEstimate(flops=1 << 18, bytes_accessed=1 << 19, transcendentals=0),
        name="spread",
    )(q)

def body(query, prompt_code_cache, prompt_scale_cache, prefix_len, sample_key_value_cache, suffix_len, w_out):
    head_width = prompt_code_cache.shape[3]
    members = lax.axis_size("prefix")
    groups = lax.axis_size("samples")

    def swap(x, axis):
        return lax.all_to_all(x, axis, split_axis=0, concat_axis=0, tiled=True)

    gathered = swap(spread(query, members, head_width), "prefix")
    keys_values, own = prep(prefix_len, suffix_len, prompt_scale_cache, prompt_code_cache, query, sample_key_value_cache)
    partials = attn(prefix_len, gathered, keys_values, own)
    attention = combine(swap(partials, "prefix"), groups)
    rows = swap(attention, "samples").reshape(-1, attention.shape[2])
    terms = jnp.dot(rows, w_out, preferred_element_type=jnp.float32).astype(jnp.bfloat16)
    terms = swap(terms.reshape(members, -1, terms.shape[1]), "prefix")
    return jnp.sum(terms.astype(jnp.float32), axis=0).astype(jnp.bfloat16)


def solution(mesh):
    in_specs = (
        P(("samples", "prefix"), None),
        P(None, "prefix", None, None),
        P(None, "prefix", None),
        P(),
        P(("samples", "prefix"), None, None, None),
        P(("samples", "prefix")),
        P("prefix", "samples"),
    )
    return jax.shard_map(body, mesh=mesh, in_specs=in_specs, out_specs=P("prefix", "samples"), check_vma=False)
```

```python
import math, functools
import jax, jax.numpy as jnp
from jax import lax
from jax.experimental import pallas as pl
from jax.experimental.pallas import tpu as pltpu
from jax.sharding import PartitionSpec as P
LOG2E = 1.4426950408889634
FLOOR = -(2.0 ** 127)

def valid_rows(plen_ref, chunk):
    return jnp.clip(plen_ref[0] - lax.axis_index("prefix") * chunk, 0, chunk)

def prep_kernel(plen_ref, len_ref, scale_ref, code_hbm, q_ref, cache_hbm, kv_hbm, own_hbm, own_ref, own_sem, code_s, cache_s, k_s, v_s, hot_s, sc_v, sc_ref, sc_sem, in_sem, cache_sem, k_sem, v_sem, *, tb, sb, cs):
    H, T, lanes = k_s.shape
    G = own_ref.shape[1] // H
    steps = k_s.shape[1] // tb

    def rows(i, size):
        return pl.ds(pl.multiple_of(i * size, size), size)

    def load(i):
        return pltpu.make_async_copy(code_hbm.at[:, rows(i, tb * H), :], code_s.at[:, rows(i, tb * H), :], in_sem.at[i])

    def save(i):
        at = rows(i, tb)
        return (pltpu.make_async_copy(k_s.at[:, at, :], kv_hbm.at[0, :, at, :], k_sem.at[i]),
                pltpu.make_async_copy(v_s.at[:, at, :], kv_hbm.at[1, :, at, :], v_sem.at[i]))

    cache_copy = pltpu.make_async_copy(cache_hbm, cache_s, cache_sem)
    load(0).start()
    cache_copy.start()
    for i in range(1, steps):
        load(i).start()
    B = scale_ref.shape[2]
    for c in range(2):
        sc_v[c * H:(c + 1) * H, 0:B] = scale_ref[c].astype(jnp.float32)
    sc_copy = pltpu.make_async_copy(sc_v, sc_ref, sc_sem)
    sc_copy.start()
    n = valid_rows(plen_ref, T)
    hr = hot_s.shape[0]
    half = sb // 2
    r = lax.broadcasted_iota(jnp.int32, (hr, hr), 0)
    c = lax.broadcasted_iota(jnp.int32, (hr, hr), 1)
    hot_s[...] = jnp.where((r % half) * H + r // half == c, 1.0, 0.0).astype(jnp.bfloat16)

    sc_copy.wait()

    @pl.loop(0, steps)
    def _(i):
        load(i).wait()
        prep_step(i, n, sc_ref, code_s, k_s, v_s, hot_s, tb=tb, sb=sb)
        for copy in save(i):
            copy.start()

    cache_copy.wait()
    q = q_ref[...].astype(jnp.float32)
    for i in range(H):
        own = jnp.concatenate([q[:, h * lanes:(h + 1) * lanes] for h in range(i * G, (i + 1) * G)], axis=0).astype(jnp.bfloat16)
        cols = slice(i * lanes, (i + 1) * lanes)
        grp = slice(i * G, (i + 1) * G)
        C = cache_s.shape[2]
        s = lax.dot_general(own, cache_s[0, 0, :, cols], (((1,), (1,)), ((), ())), preferred_element_type=jnp.float32) * cs
        s = jnp.where(lax.broadcasted_iota(jnp.int32, (G, C), 1) < len_ref[0], s, -jnp.inf)
        m = jnp.max(s, axis=1, keepdims=True)
        w = jnp.exp2(s - m).astype(jnp.bfloat16)
        own_ref[0, grp, :] = jnp.dot(w, cache_s[0, 1, :, cols], preferred_element_type=jnp.float32)
        own_ref[1, grp, :] = jnp.broadcast_to(m, (G, lanes))
        own_ref[2, grp, :] = jnp.broadcast_to(jnp.sum(w.astype(jnp.float32), axis=1, keepdims=True), (G, lanes))
    own_copy = pltpu.make_async_copy(own_ref, own_hbm.at[0:3], own_sem)
    own_copy.start()
    for i in range(steps):
        for copy in save(i):
            copy.wait()
    own_copy.wait()


def prep_step(i, n, sc_ref, code_ref, k_ref, v_ref, hot_s, *, tb, sb):
    heads = k_ref.shape[0]
    lanes = code_ref.shape[2]
    half = sb // 2
    hr = half * heads

    def move(c, b):
        x = jnp.concatenate([code_ref[c, pl.ds(pl.multiple_of(i * tb * heads, tb * heads) + (2 * b + u) * hr, hr), :] for u in range(2)], axis=1)
        y = jnp.dot(hot_s[...], x, preferred_element_type=jnp.float32)
        blk = i * (tb // sb) + b
        return [y[j * half:(j + 1) * half] * sc_ref[c * heads + j, blk] for j in range(heads)]

    def go(masked):
        for b in range(tb // sb):
            rows = [pl.ds(pl.multiple_of(i * tb, tb) + b * sb + u * half, half) for u in range(2)]
            if masked:
                left = n - i * tb - b * sb
                ok = [lax.broadcasted_iota(jnp.int32, (half, lanes), 0) + u * half < left for u in range(2)]
            for c in range(2):
                ys = move(c, b)
                if masked and c == 0 and b == 0:
                    first = [y[0:1, 0:lanes] for y in ys]
                for j in range(heads):
                    for u in range(2):
                        y = ys[j][:, u * lanes:(u + 1) * lanes]
                        if c == 0:
                            if masked:
                                y = jnp.where(ok[u], y, first[j])
                            k_ref[j, rows[u], :] = y.astype(jnp.bfloat16)
                        else:
                            if masked:
                                y = jnp.where(ok[u], y, 0.0)
                            v_ref[j, rows[u], :] = y.astype(jnp.bfloat16)

    whole = (i + 1) * tb <= n
    some = i * tb < n

    @pl.when(whole)
    def _():
        go(False)

    @pl.when(jnp.logical_and(some, jnp.logical_not(whole)))
    def _():
        go(True)

    @pl.when(jnp.logical_not(some))
    def _():
        for j in range(heads):
            k_ref[j, pl.ds(pl.multiple_of(i * tb, tb), tb), :] = jnp.broadcast_to(jnp.where(i == 0, 0.0, k_ref[j, 0:16].astype(jnp.float32)[0:1]), (tb, lanes)).astype(jnp.bfloat16)
            v_ref[j, pl.ds(pl.multiple_of(i * tb, tb), tb), :] = jnp.zeros((tb, lanes), jnp.bfloat16)

def prep(n, length, scale, code, q, cache):
    _, T, H, D = code.shape
    tb = T // 8
    sb = T // scale.shape[1]
    G = q.shape[1] // (H * D)
    smem = pl.BlockSpec(memory_space=pltpu.SMEM)
    vmem = pl.BlockSpec(memory_space=pltpu.VMEM)
    hbm = pl.BlockSpec(memory_space=pltpu.HBM)
    return pl.pallas_call(
        functools.partial(prep_kernel, tb=tb, sb=sb, cs=LOG2E / math.sqrt(D)),
        in_specs=[smem, smem, vmem, hbm, vmem, hbm],
        out_specs=[hbm, hbm],
        out_shape=[jax.ShapeDtypeStruct((4, H, T, D), jnp.bfloat16)] + [jax.ShapeDtypeStruct((480, H * G, D), jnp.float32)],
        scratch_shapes=[pltpu.VMEM((3, H * G, D), jnp.float32), pltpu.SemaphoreType.DMA, pltpu.VMEM((2, T * H, D), jnp.bfloat16), pltpu.VMEM(cache.shape, jnp.bfloat16),
                        pltpu.VMEM((H, T, D), jnp.bfloat16), pltpu.VMEM((H, T, D), jnp.bfloat16),
                        pltpu.VMEM((sb // 2 * H, sb // 2 * H), jnp.bfloat16),
                        pltpu.VMEM((2 * H, 128), jnp.float32), pltpu.SMEM((2 * H, 128), jnp.float32), pltpu.SemaphoreType.DMA,
                        pltpu.SemaphoreType.DMA((T // tb,)), pltpu.SemaphoreType.DMA,
                        pltpu.SemaphoreType.DMA((T // tb,)), pltpu.SemaphoreType.DMA((T // tb,))],
        compiler_params=pltpu.CompilerParams(vmem_limit_bytes=63_300_000),
        cost_estimate=pl.CostEstimate(flops=16 << 20, bytes_accessed=20 << 20, transcendentals=0),
        name="prep",
    )(n, length, scale.transpose(0, 2, 1), code.reshape(2, T * H, D), q, cache)

def attn_kernel(plen_ref, qg_ref, kv_hbm, own_hbm, out_ref, own_ref, own_sem, q_s, k_ref, v_ref, one_s, k_sem, v_sem, *s_s, cs, tile, nbuf):
    S, HQ, D = qg_ref.shape
    _, H, T, _ = kv_hbm.shape
    G = HQ // H
    n = valid_rows(plen_ref, T)
    me = lax.axis_index("prefix")
    R = G * S
    hp = 64 // S
    load_k = [pltpu.make_async_copy(kv_hbm.at[0, j], k_ref.at[j], k_sem.at[j]) for j in range(H)]
    load_v = [pltpu.make_async_copy(kv_hbm.at[1, j], v_ref.at[j], v_sem.at[j]) for j in range(H)]
    load_own = pltpu.make_async_copy(own_hbm.at[0:3], own_ref, own_sem)
    load_k[0].start()
    load_k[1].start()
    load_v[0].start()
    load_own.start()
    one_s[...] = jnp.where(lax.broadcasted_iota(jnp.int32, (T, D), 0) < n, 1.0, 0.0).astype(jnp.bfloat16)
    sidx = lax.broadcasted_iota(jnp.int32, (S, D), 0)
    q_s[...] = qg_ref[...].astype(jnp.float32).reshape(S * HQ, D)
    ms = {}
    def scores(j, c):
        if c == 0:
            q = jnp.concatenate([q_s[pl.ds(j * G + h, S, stride=HQ), :] for h in range(G)], axis=0).astype(jnp.bfloat16)
            ms[j] = [q, None]
        q = ms[j][0]
        z = lax.dot_general(q, k_ref[j, c * tile:(c + 1) * tile, :], (((1,), (1,)), ((), ())), preferred_element_type=jnp.float32)
        s_s[j % nbuf][:, c * tile:(c + 1) * tile] = z
        m = ms[j][1]
        for l in range(tile // D):
            zz = z[:, l * D:(l + 1) * D]
            m = zz if m is None else jnp.maximum(m, zz)
        ms[j][1] = m
        if (c + 1) * tile == T:
            m = jnp.max(m, axis=1, keepdims=True) * cs
            ms[j][1] = jnp.broadcast_to(m, (R, D)).astype(jnp.bfloat16).astype(jnp.float32)
    acc = {}
    part = {}
    def weigh(j, c):
        half = R // 2
        wide = 2 * tile
        h, cc = c % 2, c // 2
        m = ms[j][1][h * half:(h + 1) * half]
        at = slice(cc * wide, (cc + 1) * wide)
        z = s_s[j % nbuf][h * half:(h + 1) * half, at]
        p = jnp.exp2(z * cs - jnp.concatenate([m] * (wide // D), axis=1)).astype(jnp.bfloat16)
        o = jnp.dot(p, jnp.concatenate([v_ref[j, at, :], one_s[at, :]], axis=1), preferred_element_type=jnp.float32)
        part[(j, h)] = o if cc == 0 else part[(j, h)] + o
        if (c + 1) * tile == T:
            acc[j] = jnp.concatenate([part[(j, 0)], part[(j, 1)]], axis=0)
    def finish(j):
        o = acc[j][:, :D]
        tot = acc[j][:, D:]
        m = jnp.where(n > 0, ms[j][1], FLOOR)
        mts = []
        for h in range(G):
            sl = slice(h * S, (h + 1) * S)
            r = j * G + h
            mine = sidx == me
            sm2 = jnp.where(mine, own_ref[1, r:r + 1, :], FLOOR)
            mn = jnp.maximum(m[sl], sm2).astype(jnp.bfloat16).astype(jnp.float32)
            fa = jnp.exp2(m[sl] - mn)
            fb = jnp.where(mine, jnp.exp2(sm2 - mn), 0.0)
            on = o[sl] * fa + own_ref[0, r:r + 1, :] * fb
            tn = tot[sl] * fa + own_ref[2, r:r + 1, :] * fb
            d, hd = divmod(r, hp)
            out_ref[d, hd * S:(hd + 1) * S, :] = on.astype(jnp.bfloat16)
            mts.append((mn, tn))
        diag = lax.broadcasted_iota(jnp.int32, (64, D), 0) == lax.broadcasted_iota(jnp.int32, (64, D), 1)
        for d0 in range(G // hp):
            mm = jnp.concatenate([a for a, _ in mts[d0 * hp:(d0 + 1) * hp]], axis=0)
            tt = jnp.concatenate([b for _, b in mts[d0 * hp:(d0 + 1) * hp]], axis=0)
            mr = jnp.sum(jnp.where(diag, mm, 0.0), axis=0, keepdims=True)
            tr = jnp.sum(jnp.where(diag, tt, 0.0), axis=0, keepdims=True)
            hi = tr.astype(jnp.bfloat16).astype(jnp.float32)
            st = jnp.concatenate([mr, hi, tr - hi, jnp.zeros((5, D), jnp.float32)], axis=0)
            out_ref[j * (G // hp) + d0, 64:72, :] = st.astype(jnp.bfloat16)
    nt = T // tile
    K = lambda *a: [('k', i) for i in a]
    V = lambda *a: [('v', i) for i in a]
    waits = {0: K(0), 1: K(1) + V(0), 2: K(2, 3) + V(1, 2), 4: K(4, 5) + V(3, 4), 6: K(6, 7) + V(5, 6, 7)}
    plan = {0: K(2, 3) + V(1, 2), 1: K(4, 5) + V(3, 4), 3: K(6, 7) + V(5, 6, 7)}
    for j in range(H + 1):
        for c in range(nt):
            if j < H:
                if c == 0:
                    if j == 1:
                        load_own.wait()
                    for which, i in waits.get(j, ()):
                        (load_k if which == 'k' else load_v)[i].wait()
                    for which, i in plan.get(j, ()):
                        (load_k if which == 'k' else load_v)[i].start()
                scores(j, c)
            if j == H and c == 0:
                for which, i in waits.get(j, ()):
                    (load_k if which == 'k' else load_v)[i].wait()
            if j > 0:
                weigh(j - 1, c)
        if j > 0:
            finish(j - 1)

def attn(n, qg, kv, own, tile=256, nbuf=2):
    S, HQ, D = qg.shape
    _, H, T, _ = kv.shape
    nd = HQ * S // 64
    vm = pl.BlockSpec(memory_space=pltpu.VMEM)
    hbm = pl.BlockSpec(memory_space=pltpu.HBM)
    return pl.pallas_call(
        functools.partial(attn_kernel, cs=LOG2E / math.sqrt(D), tile=tile, nbuf=nbuf),
        in_specs=[pl.BlockSpec(memory_space=pltpu.SMEM), vm, hbm, hbm],
        out_specs=vm,
        out_shape=jax.ShapeDtypeStruct((nd, 72, D), jnp.bfloat16),
        scratch_shapes=[pltpu.VMEM((3,) + own.shape[1:], own.dtype), pltpu.SemaphoreType.DMA, pltpu.VMEM((S * HQ, D), jnp.float32), pltpu.VMEM((H, T, D), jnp.bfloat16), pltpu.VMEM((H, T, D), jnp.bfloat16), pltpu.VMEM((T, D), jnp.bfloat16),
                        pltpu.SemaphoreType.DMA((H,)), pltpu.SemaphoreType.DMA((H,))] + [pltpu.VMEM((S * HQ // H, T), jnp.float32)] * nbuf,
        compiler_params=pltpu.CompilerParams(vmem_limit_bytes=48_000_000),
        cost_estimate=pl.CostEstimate(flops=2 << 30, bytes_accessed=12 << 20, transcendentals=4 << 20),
        name="attn",
    )(n, qg, kv, own)

def combine_kernel(r_ref, o_ref, st_s):
    B = r_ref.shape[0]
    D = r_ref.shape[2]
    st_s[...] = r_ref[:, 64:72, :].astype(jnp.float32).reshape(B * 8, D)
    m = st_s[pl.ds(0, B, stride=8), :]
    t = st_s[pl.ds(1, B, stride=8), :] + st_s[pl.ds(2, B, stride=8), :]
    M = jnp.max(m, axis=0, keepdims=True)
    f = jnp.exp2(m - M)
    den = jnp.sum(f * t, axis=0, keepdims=True)
    lane = lax.broadcasted_iota(jnp.int32, (B, D), 1)
    f = jnp.where(lane < 64, f / den, 0.0)
    ft = jnp.transpose(jnp.concatenate([f, jnp.zeros((D - B, D), jnp.float32)], axis=0))[:64]
    acc = jnp.zeros((64, D), jnp.float32)
    for b in range(B):
        acc = acc + r_ref[b, 0:64, :].astype(jnp.float32) * ft[:, b:b + 1]
    res = jnp.concatenate([acc[:32], acc[32:]], axis=1).astype(jnp.bfloat16)
    for g in range(o_ref.shape[0]):
        o_ref[g] = res

def combine(r, copies):
    B, _, D = r.shape
    return pl.pallas_call(
        combine_kernel,
        in_specs=[pl.BlockSpec(memory_space=pltpu.VMEM)],
        out_specs=pl.BlockSpec(memory_space=pltpu.VMEM),
        out_shape=jax.ShapeDtypeStruct((copies, 32, 2 * D), jnp.bfloat16),
        scratch_shapes=[pltpu.VMEM((B * 8, D), jnp.float32)],
        compiler_params=pltpu.CompilerParams(vmem_limit_bytes=10 << 20),
        cost_estimate=pl.CostEstimate(flops=1 << 20, bytes_accessed=1 << 20, transcendentals=0),
        name="combine",
    )(r)

def spread_kernel(q_hbm, o_hbm, q_ref, x_ref, q_sem, o_sem):
    M, HQ, D = o_hbm.shape
    load = pltpu.make_async_copy(q_hbm, q_ref, q_sem)
    load.start()
    load.wait()
    q = q_ref[...].astype(jnp.float32)
    x = jnp.concatenate([q[:, h * D:(h + 1) * D] for h in range(HQ)], axis=0).astype(jnp.bfloat16)
    part = x_ref.shape[0]
    for i in range(part):
        x_ref[i] = x
    copies = [pltpu.make_async_copy(x_ref, o_hbm.at[i * part:(i + 1) * part], o_sem.at[i]) for i in range(M // part)]
    for copy in copies:
        copy.start()
    for copy in copies:
        copy.wait()

def spread(q, members, width):
    hbm = pl.BlockSpec(memory_space=pltpu.HBM)
    rows = q.shape[1] // width
    return pl.pallas_call(
        spread_kernel, in_specs=[hbm], out_specs=hbm,
        out_shape=jax.ShapeDtypeStruct((members, rows, width), q.dtype),
        scratch_shapes=[pltpu.VMEM(q.shape, q.dtype), pltpu.VMEM((8, rows, width), q.dtype),
                        pltpu.SemaphoreType.DMA, pltpu.SemaphoreType.DMA((members // 8,))],
        compiler_params=pltpu.CompilerParams(vmem_limit_bytes=63_480_000),
        cost_estimate=pl.CostEstimate(flops=1 << 18, bytes_accessed=1 << 19, transcendentals=0),
        name="spread",
    )(q)

def body(query, prompt_code_cache, prompt_scale_cache, prefix_len, sample_key_value_cache, suffix_len, w_out):
    head_width = prompt_code_cache.shape[3]
    members = lax.axis_size("prefix")
    groups = lax.axis_size("samples")

    def swap(x, axis):
        return lax.all_to_all(x, axis, split_axis=0, concat_axis=0, tiled=True)

    gathered = swap(spread(query, members, head_width), "prefix")
    keys_values, own = prep(prefix_len, suffix_len, prompt_scale_cache, prompt_code_cache, query, sample_key_value_cache)
    partials = attn(prefix_len, gathered, keys_values, own)
    attention = combine(swap(partials, "prefix"), groups)
    rows = swap(attention, "samples").reshape(-1, attention.shape[2])
    terms = jnp.dot(rows, w_out, preferred_element_type=jnp.float32).astype(jnp.bfloat16)
    terms = swap(terms.reshape(members, -1, terms.shape[1]), "prefix")
    return jnp.sum(terms.astype(jnp.float32), axis=0).astype(jnp.bfloat16)


def solution(mesh):
    in_specs = (
        P(("samples", "prefix"), None),
        P(None, "prefix", None, None),
        P(None, "prefix", None),
        P(),
        P(("samples", "prefix"), None, None, None),
        P(("samples", "prefix")),
        P("prefix", "samples"),
    )
    return jax.shard_map(body, mesh=mesh, in_specs=in_specs, out_specs=P("prefix", "samples"), check_vma=False)
```
